32 devices in a mesh: groups: 2 (over x), replica: 2 (over core), tensor: 8 (over z, y).
Axes of the slice: x: 2, y: 2, z: 4, core: 2. Of those that a mesh axis runs over, the one named last changes fastest.
Arguments:
- queries: bfloat16 [2, 64, 8192], P(None, ('groups', 'replica'), 'tensor'), parts along dimension 1, may hold values from -8 to 8
- latest_key_value: bfloat16 [2, 64, 8, 256], P(None, ('groups', 'replica'), 'tensor'), parts along dimension 1, may hold values from -6 to 6, as said below
- residual: bfloat16 [2, 64, 8192], P(None, ('groups', 'replica'), 'tensor'), parts along dimension 1, may hold values from -3 to 3
- paged_cache_pool: bfloat16 [512, 8, 64, 256], P(('groups', 'replica'), 'tensor'), parts along dimension 0, may hold values from -6 to 6, as said below
- adapter_down_weight: bfloat16 [16, 64, 8192], P(('groups', 'replica'), None, 'tensor'), parts along dimension 0, may hold values from -0.5 to 0.5
- adapter_up_weight: bfloat16 [16, 64, 8192], P(('groups', 'replica'), None, 'tensor'), parts along dimension 0, may hold values from -0.375 to 0.375
- output_weight: bfloat16 [8192, 8192], P('tensor'), may hold values from -0.5 to 0.5
- lengths: int32 [64], P('groups'), parts along dimension 0, may hold values from 1 to 512, as said below
- previous_block_table: int32 [64, 8], P('groups'), parts along dimension 0, may hold values from 0 to 127, as said below
- request_order_after: int32 [64], P('groups'), parts along dimension 0, may hold values from 0 to 31, as said below
- request_adapter_index: int32 [64], P('groups'), parts along dimension 0, may hold values from 0 to 3
Outputs:
- layer_out: bfloat16 [2, 64, 8192], P(None, ('groups', 'replica'), 'tensor'), parts along dimension 1
- placed_cache: bfloat16 [64, 8, 8, 64, 256], P(('groups', 'replica'), None, 'tensor'), parts along dimension 0
The draws below stay inside these ranges and needn't reach their ends.
There are 2 independent parts, one for each index of `groups`. The reference program is written for one: setup_inputs(seed, part) draws one part's arguments, and reference() takes and returns one part's arrays. A program takes and returns all parts, laid end to end along the dimension named above; an argument that names none is the same for every part. Nothing has to cross between parts.
Inputs may be any that keep to these rules, and one draw needn't show every extreme that they name: `lengths`: request 0 has exactly 512. `previous_block_table`: block numbers in the holder's own pool; the blocks of the 16 requests of one replica are all different. `request_order_after`: A permutation; of the 16 requests at the new places of each replica exactly 8 are held by another replica. `request_adapter_index`: A slot of the holder's own adapter pool. `paged_cache_pool`: each key and value head is stored in 1 equal copies, side by side. `latest_key_value`: each key and value head is given in 1 equal copies, side by side.
All inputs are finite; a program needn't handle non-finite values.
Results may differ from the reference program's by a relative error of at most 0.006.
Values may be sent and summed in bfloat16 or wider, within the bound.
No kernel may reach another device: no remote copies, remote signals or barrier semaphores. Data moves between devices by JAX's collectives and lax.ppermute only.
A program may use at most 128 MiB of HBM per device.

```python
import jax
import jax.numpy as jnp
from jax import lax

MODEL_WIDTH = 8192
QUERY_HEADS = 64
KVH = 8
HEAD_WIDTH = 128
ADAPTER_RANK = 64
STEPS = 2
BLOCK = 64
MAXB = 8
R_DEV = 16
ADP_DEV = 4
LMAX = 512
POOL_DEV = 128
POOL_ALL = 256
REQS = 32
ADAPTER_TOTAL = 8
KV_SLOTS = 8


def request_layout(key):
    replicas = REQS // R_DEV
    half_rows = R_DEV // 2
    long_lengths = jax.random.randint(jax.random.fold_in(key, 101), (replicas, R_DEV), LMAX // 2, LMAX + 1)
    short_lengths = jax.random.randint(jax.random.fold_in(key, 102), (replicas, R_DEV), 1, LMAX // 4 + 1)
    even_rank = (jnp.arange(replicas) % 2 == 0)[:, None]
    all_lengths = jnp.where(even_rank, long_lengths, short_lengths).reshape(REQS)
    all_lengths = all_lengths.at[0].set(LMAX).astype(jnp.int32)
    table_keys = jax.random.split(jax.random.fold_in(key, 103), replicas)
    tables = jax.vmap(lambda part_key: jax.random.permutation(part_key, POOL_DEV))(table_keys)
    tables = tables.reshape(REQS, MAXB).astype(jnp.int32)
    order_keys = jax.random.split(jax.random.fold_in(key, 104), replicas)
    orders = jax.vmap(lambda part_key: jax.random.permutation(part_key, R_DEV))(order_keys)
    orders = orders + (jnp.arange(replicas) * R_DEV)[:, None]
    staying = orders[:, :half_rows]
    leaving = orders[:, half_rows:]
    partner = jnp.bitwise_xor(jnp.arange(replicas), 1)
    landed_requests = jnp.concatenate([staying, leaving[partner]], axis=1)
    shuffle_keys = jax.random.split(jax.random.fold_in(key, 105), replicas)
    shuffles = jax.vmap(lambda part_key: jax.random.permutation(part_key, R_DEV))(shuffle_keys)
    placed_order = jnp.take_along_axis(landed_requests, shuffles, axis=1).reshape(REQS).astype(jnp.int32)
    return (all_lengths, tables, placed_order)


def draw_lengths(key, part):
    return request_layout(key)[0]


def draw_previous_block_table(key, part):
    return request_layout(key)[1]


def draw_request_order_after(key, part):
    return request_layout(key)[2]


def draw_paged_cache_pool(key, part):
    key = jax.random.fold_in(key, 3)
    shape = (POOL_ALL, KVH, BLOCK, 2 * HEAD_WIDTH)
    sample = jax.random.truncated_normal(key, -6.0, 6.0, shape, jnp.float32)
    sample = jnp.repeat(sample, KV_SLOTS // KVH, axis=1)
    return sample.astype(jnp.bfloat16)


def draw_latest_key_value(key, part):
    key = jax.random.fold_in(key, 5)
    shape = (STEPS, REQS, KVH, 2 * HEAD_WIDTH)
    sample = 2.0 * jax.random.truncated_normal(key, -3.0, 3.0, shape, jnp.float32)
    sample = jnp.repeat(sample, KV_SLOTS // KVH, axis=2)
    return sample.astype(jnp.bfloat16)


def draw_queries(key, part):
    key = jax.random.fold_in(key, 7)
    shape = (STEPS, REQS, QUERY_HEADS, HEAD_WIDTH)
    sample = jax.random.truncated_normal(key, -6.0, 6.0, shape, jnp.float32)
    return sample.reshape(STEPS, REQS, QUERY_HEADS * HEAD_WIDTH).astype(jnp.bfloat16)


def place_ends(values, key, low, largest):
    shape = values.shape
    spot = [jax.random.randint(jax.random.fold_in(key, axis), (), 0, shape[axis]) for axis in range(len(shape))]
    values = values.at[tuple(spot)].set(low)
    longest = shape.index(max(shape))
    spot[longest] = (spot[longest] + 1) % shape[longest]
    return values.at[tuple(spot)].set(largest)


def block_levels(rng, shape, cuts, low, top_value):
    factor_of = 1.0
    for position, blocks in cuts:
        steps = jax.random.uniform(jax.random.fold_in(jax.random.fold_in(rng, 6), position), (blocks,), jnp.float32, low / len(cuts), top_value / len(cuts))
        factor_of = factor_of * jnp.repeat(jnp.exp(steps), shape[position] // blocks).reshape((-1,) + (1,) * (len(shape) - 1 - position))
    return factor_of


def centred(rng, shape, width, limit, pieces=(), held_as=jnp.bfloat16):
    array = jax.random.normal(rng, shape, jnp.float32) * width
    if len(pieces) > 0:
        array = block_levels(rng, shape, pieces, -0.22, 0.18) * array
    return jnp.clip(array, min=-limit, max=limit).astype(held_as)


def setup_inputs(seed: int = 0, part: int = 0) -> dict:
    seeds = jax.random.split(jax.random.key(seed), 12)
    part_keys = jax.random.split(jax.random.fold_in(seeds[11], part), 12)
    return {
        "queries": draw_queries(jax.random.fold_in(jax.random.fold_in(seeds[11], part), 71), part),
        "latest_key_value": draw_latest_key_value(jax.random.fold_in(jax.random.fold_in(seeds[11], part), 71), part),
        "residual": centred(part_keys[2], (STEPS, REQS, MODEL_WIDTH), 0.5, 3.0, ((1, 2), (2, 8))),
        "paged_cache_pool": draw_paged_cache_pool(jax.random.fold_in(jax.random.fold_in(seeds[11], part), 71), part),
        "adapter_down_weight": centred(part_keys[4], (ADAPTER_TOTAL, ADAPTER_RANK, QUERY_HEADS * HEAD_WIDTH), HEAD_WIDTH ** -0.5, 0.5, ((0, 2), (2, 8))),
        "adapter_up_weight": centred(part_keys[5], (ADAPTER_TOTAL, ADAPTER_RANK, MODEL_WIDTH), (4 * ADAPTER_RANK) ** -0.5, 0.375, ((0, 2), (2, 8))),
        "output_weight": centred(seeds[6], (QUERY_HEADS * HEAD_WIDTH, MODEL_WIDTH), HEAD_WIDTH ** -0.5, 0.5, ((0, 8),)),
        "lengths": draw_lengths(jax.random.fold_in(jax.random.fold_in(seeds[11], part), 71), part),
        "previous_block_table": draw_previous_block_table(jax.random.fold_in(jax.random.fold_in(seeds[11], part), 71), part),
        "request_order_after": draw_request_order_after(jax.random.fold_in(jax.random.fold_in(seeds[11], part), 71), part),
        "request_adapter_index": place_ends(jax.random.randint(part_keys[10], (REQS,), 0, ADP_DEV), jax.random.fold_in(part_keys[10], 1), 0, ADP_DEV - 1).astype(jnp.int32),
    }


adapter_scale = 2.0


def attend_one(query_row, cache_rows, length, fresh_rows):
    stored = cache_rows.shape[1]
    group_size = QUERY_HEADS // stored
    head_query = query_row.astype(jnp.float32).reshape(stored, group_size, HEAD_WIDTH)
    cache_float = cache_rows.astype(jnp.float32)
    scale = HEAD_WIDTH ** -0.5
    scores = jnp.einsum("sgd,bstd->sgbt", head_query, cache_float[..., :HEAD_WIDTH]) * scale
    positions = jnp.arange(MAXB, dtype=jnp.int32)[:, None] * BLOCK + jnp.arange(BLOCK, dtype=jnp.int32)[None, :]
    inside = positions < length
    scores = jnp.where(inside[None, None], scores, jnp.float32(-1e30))
    fresh_scores = [jnp.einsum("sgd,sd->sg", head_query, row[..., :HEAD_WIDTH].astype(jnp.float32)) * scale for row in fresh_rows]
    top_score = jnp.max(scores, axis=(2, 3))
    for extra in fresh_scores:
        top_score = jnp.maximum(top_score, extra)
    weights = jnp.exp(scores - top_score[..., None, None])
    fresh_weights = [jnp.exp(extra - top_score) for extra in fresh_scores]
    totals = jnp.sum(weights, axis=(2, 3))
    for extra in fresh_weights:
        totals = totals + extra
    probabilities = (weights / totals[..., None, None]).astype(jnp.bfloat16)
    attended = jnp.einsum("sgbt,bstd->sgd", probabilities.astype(jnp.float32), cache_float[..., HEAD_WIDTH:])
    for extra, row in zip(fresh_weights, fresh_rows):
        share = lax.optimization_barrier((extra / totals).astype(jnp.bfloat16)).astype(jnp.float32)
        attended = attended + share[..., None] * row[:, None, HEAD_WIDTH:].astype(jnp.float32)
    return attended.reshape(QUERY_HEADS * HEAD_WIDTH).astype(jnp.bfloat16)


def reference(queries, latest_key_value, residual, paged_cache_pool, adapter_down_weight, adapter_up_weight, output_weight, lengths, previous_block_table, request_order_after, request_adapter_index):
    holder = request_order_after // R_DEV
    new_lengths = lengths[request_order_after]

    def place(index):
        request = request_order_after[index]
        blocks = (holder[index] * POOL_DEV + previous_block_table[request]).astype(jnp.int32)
        rows_here = paged_cache_pool[blocks]
        positions = jnp.arange(MAXB, dtype=jnp.int32)[:, None] * BLOCK + jnp.arange(BLOCK, dtype=jnp.int32)[None, :]
        inside = positions < lengths[request]
        return jnp.where(inside[:, None, :, None], rows_here, jnp.zeros_like(rows_here))

    placed = lax.map(place, jnp.arange(REQS, dtype=jnp.int32))
    overall_adapter_index = (holder * ADP_DEV + request_adapter_index[request_order_after]).astype(jnp.int32)
    lowered_rows = adapter_down_weight[overall_adapter_index].astype(jnp.float32)
    raised_rows = adapter_up_weight[overall_adapter_index].astype(jnp.float32)
    results = []
    for decode_step_index in range(STEPS):
        step_queries = queries[decode_step_index][request_order_after]
        fresh = jnp.moveaxis(latest_key_value[: decode_step_index + 1][:, request_order_after], 0, 1)

        def serve(items):
            query_row, cache_rows, length, fresh_rows = items
            return attend_one(query_row, cache_rows, length, [fresh_rows[k] for k in range(decode_step_index + 1)])

        attended = lax.map(serve, (step_queries, placed, new_lengths, fresh))
        output_projected = jnp.dot(attended, output_weight, preferred_element_type=jnp.float32)
        shrink = jnp.einsum("rc,rkc->rk", attended.astype(jnp.float32), lowered_rows).astype(jnp.bfloat16)
        widen_back = jnp.einsum("rk,rkc->rc", shrink.astype(jnp.float32), raised_rows)
        combined_output = residual[decode_step_index][request_order_after].astype(jnp.float32) + output_projected + adapter_scale * widen_back
        results.append(combined_output.astype(jnp.bfloat16))
    return jnp.stack(results), placed
```

```python
import jax
import jax.numpy as jnp
from jax import lax
from jax.experimental import pallas as pl
from jax.experimental.pallas import tpu as pltpu
from jax.sharding import PartitionSpec as P

adapter_scale = 2.0
bf16 = jnp.bfloat16
f32 = jnp.float32
LANES = 128
VMEM_BYTES = 56 * 1024 * 1024


def iota(shape, dim):
    return lax.broadcasted_iota(jnp.int32, shape, dim)


def div(value, size):
    return value >> (size.bit_length() - 1) if size & (size - 1) == 0 else value // size


def mod(value, size):
    return value & (size - 1) if size & (size - 1) == 0 else value % size


def dot(a, b, contract=((1,), (0,))):
    return lax.dot_general(a, b, (contract, ((), ())), preferred_element_type=f32)


def one_hot(mask):
    return jnp.where(mask, 1.0, 0.0).astype(bf16)


def rank_rows(order_ref, found_ref, holder, place, row_count, base):
    def step(j, count):
        request = order_ref[place * row_count + j]
        hit = div(request, row_count) == holder

        @pl.when(hit)
        def _():
            found_ref[base + count] = request - holder * row_count

        return count + hit.astype(jnp.int32)

    lax.fori_loop(0, row_count, step, jnp.int32(0))


def attend_kernel(
    order_ref,
    lengths_ref,
    table_ref,
    adapter_ref,
    queries_hbm,
    fresh_hbm,
    down_hbm,
    pool_ref,
    weight_ref,
    send_ref,
    queries_ref,
    fresh_ref,
    down_ref,
    pool_v,
    weight_v,
    scores_v,
    probs_v,
    attended_v,
    send_v,
    found,
    small_sem,
    pool_sem,
    weight_sem,
    send_sem,
):
    steps, rows, features = queries_ref.shape
    blocks, block_size, width = pool_v.shape
    head = width // 2
    heads = features // head
    sh = steps * heads
    table_blocks = table_ref.shape[0]
    positions = table_blocks * block_size
    places = lengths_ref.shape[0] // rows
    half = rows // places
    tensor = weight_v.shape[0]
    slots, rank = down_ref.shape[:2]
    me = lax.axis_index("replica")
    first = me * rows

    small_copies = [
        pltpu.make_async_copy(source, target, small_sem.at[n])
        for n, (source, target) in enumerate(
            ((queries_hbm, queries_ref), (fresh_hbm, fresh_ref), (down_hbm, down_ref))
        )
    ]
    pool_copy = pltpu.make_async_copy(pool_ref, pool_v, pool_sem)
    out_width = weight_v.shape[2]
    weight_copies = [
        pltpu.make_async_copy(
            weight_ref.at[:, pl.ds(t * out_width, out_width)], weight_v.at[t], weight_sem.at[t]
        )
        for t in range(tensor)
    ]
    small_copies[0].start()
    small_copies[1].start()
    pool_copy.start()
    small_copies[2].start()
    for copy in weight_copies[:2]:
        copy.start()

    for place in range(places):
        rank_rows(order_ref, found, me, place, rows, place * half)

    small_copies[0].wait()
    small_copies[1].wait()
    stacked = jnp.concatenate(
        [
            queries_ref[s, :, h * head : (h + 1) * head]
            for s in range(steps)
            for h in range(heads)
        ],
        axis=0,
    )
    total = rows * sh
    out_row, in_row = iota((total, total), 0), iota((total, total), 1)
    turn = one_hot((div(out_row, sh) == mod(in_row, rows)) & (mod(out_row, sh) == div(in_row, rows)))
    turned = dot(turn, stacked)
    query_rows = turned.astype(bf16)
    spread = one_hot(div(iota((total, rows), 0), sh) == iota((total, rows), 1))
    scale = head ** (-0.5)
    fresh_rows = [dot(spread, fresh_ref[s]) for s in range(steps)]
    step_of = div(mod(iota((total, 1), 0), sh), heads)
    fresh_scores = []
    for s in range(steps):
        value = jnp.sum(turned * fresh_rows[s][:, :head], axis=1, keepdims=True) * scale
        fresh_scores.append(jnp.where(step_of >= s, value, f32(-1e30)))

    pool_copy.wait()
    for copy in weight_copies[2:]:
        copy.start()

    def block_rows(row, lo):
        return jnp.concatenate(
            [pool_v[table_ref[b, first + row], :, lo : lo + head] for b in range(table_blocks)],
            axis=0,
        )

    column = iota((sh, positions), 1)
    for row in range(rows):
        part = dot(query_rows[row * sh : (row + 1) * sh], block_rows(row, 0), ((1,), (1,)))
        part = jnp.where(column < lengths_ref[first + row], part * scale, f32(-1e30))
        scores_v[row * sh : (row + 1) * sh, :] = part

    scores = scores_v[...]
    top = jnp.max(scores, axis=1, keepdims=True)
    for value in fresh_scores:
        top = jnp.maximum(top, value)
    weights = jnp.exp(scores - top)
    fresh_weights = [jnp.exp(value - top) for value in fresh_scores]
    totals = jnp.sum(weights, axis=1, keepdims=True)
    for value in fresh_weights:
        totals = totals + value
    probs_v[...] = weights / totals

    for row in range(rows):
        span = slice(row * sh, (row + 1) * sh)
        attended_v[span, :] = dot(probs_v[span, :].astype(bf16), block_rows(row, head))
    attended = attended_v[...]
    for value, row in zip(fresh_weights, fresh_rows):
        share = (value / totals).astype(bf16).astype(f32)
        attended = attended + share * row[:, head:]
    attended = attended.astype(bf16)

    row_index = iota((places * steps * half, 1), 0)
    source = jnp.zeros_like(row_index)
    adapter = jnp.zeros_like(row_index)
    for place in range(places):
        for slot in range(half):
            local = found[place * half + slot]
            here = (div(row_index, steps * half) == place) & (mod(row_index, half) == slot)
            source = jnp.where(here, local, source)
            adapter = jnp.where(here, adapter_ref[first + local], adapter)
    step_index = div(mod(row_index, steps * half), half)
    columns = iota((places * steps * half, total), 1)
    pieces = []
    for h in range(heads):
        wanted = source * sh + step_index * heads + h
        pieces.append(dot(one_hot(columns == wanted), attended))
    mixed = jnp.concatenate(pieces, axis=1).astype(bf16)

    small_copies[2].wait()
    wide = dot(mixed, down_ref[...].reshape(slots * rank, features), ((1,), (1,)))
    shrink = jnp.zeros((places * steps * half, rank), f32)
    for slot in range(slots):
        shrink = shrink + jnp.where(
            adapter == slot, wide[:, slot * rank : (slot + 1) * rank], 0.0
        )
    shrink = jnp.concatenate(
        [shrink, jnp.zeros((places * steps * half, LANES - rank), f32)], axis=1
    ).astype(bf16)

    group = steps * half
    send_copies = []
    for t in range(tensor):
        weight_copies[t].wait()
        projected = dot(mixed, weight_v[t]).astype(bf16)
        for place in range(places):
            span = slice(place * group, (place + 1) * group)
            send_v[t, place, :, :out_width] = projected[span]
            send_v[t, place, :, out_width:] = shrink[span]
            copy = pltpu.make_async_copy(
                send_v.at[t, place], send_ref.at[place, t], send_sem.at[t, place]
            )
            copy.start()
            send_copies.append(copy)
    for copy in send_copies:
        copy.wait()


def attend_call(order, lengths, table, adapters, queries, fresh, down, pool, weight):
    steps, rows, features = queries.shape
    replicas = lax.axis_size("replica")
    tensor = lax.axis_size("tensor")
    blocks, block_size, width = pool.shape
    positions = table.shape[0] * block_size
    score_rows = rows * steps * features // (width // 2)
    out_width = weight.shape[1] // tensor
    smem = pl.BlockSpec(memory_space=pltpu.SMEM)
    hbm = pl.BlockSpec(memory_space=pl.ANY)
    return pl.pallas_call(
        attend_kernel,
        out_shape=jax.ShapeDtypeStruct(
            (replicas, tensor, steps * rows // replicas, out_width + LANES), bf16
        ),
        in_specs=[smem] * 4 + [hbm] * 5,
        out_specs=hbm,
        scratch_shapes=[
            pltpu.VMEM(queries.shape, bf16),
            pltpu.VMEM(fresh.shape, bf16),
            pltpu.VMEM(down.shape, bf16),
            pltpu.VMEM((blocks, block_size, width), bf16),
            pltpu.VMEM((tensor, weight.shape[0], out_width), bf16),
            pltpu.VMEM((score_rows, positions), f32),
            pltpu.VMEM((score_rows, positions), f32),
            pltpu.VMEM((score_rows, width // 2), f32),
            pltpu.VMEM((tensor, replicas, steps * rows // replicas, out_width + LANES), bf16),
            pltpu.SMEM((rows,), jnp.int32),
            pltpu.SemaphoreType.DMA((3,)),
            pltpu.SemaphoreType.DMA,
            pltpu.SemaphoreType.DMA((tensor,)),
            pltpu.SemaphoreType.DMA((tensor, replicas)),
        ],
        compiler_params=pltpu.CompilerParams(vmem_limit_bytes=VMEM_BYTES),
        name="attend",
    )(order, lengths, table, adapters, queries, fresh, down, pool, weight)


def place_kernel(
    order_ref,
    lengths_ref,
    table_ref,
    adapter_ref,
    own_ref,
    other_ref,
    residual_ref,
    other_residual_ref,
    out_ref,
    base_ref,
    mix_ref,
    slot_ref,
    blocks_v,
    block_sem,
    out_sem,
):
    rows, table_blocks, block_size, width = blocks_v.shape
    steps, _, features = residual_ref.shape
    group = mix_ref.shape[0] // 2
    half = group // steps
    tensor = mix_ref.shape[1] // (2 * group)
    me = lax.axis_index("replica")

    def fetch(j, carry):
        request = order_ref[me * rows + j]
        mine = div(request, rows) == me

        @pl.when(mine)
        def _():
            for b in range(table_blocks):
                source = own_ref.at[table_ref[b, request]]
                pltpu.make_async_copy(source, blocks_v.at[j, b], block_sem.at[j]).start()

        @pl.when(jnp.logical_not(mine))
        def _():
            for b in range(table_blocks):
                source = other_ref.at[table_ref[b, request]]
                pltpu.make_async_copy(source, blocks_v.at[j, b], block_sem.at[j]).start()

        return carry

    lax.fori_loop(0, rows, fetch, 0)

    out_row = iota((steps * rows, 1), 0)
    step_of, place_of = div(out_row, rows), mod(out_row, rows)
    landed_row = jnp.zeros_like(out_row)
    residual_row = jnp.zeros_like(out_row)
    slot = jnp.zeros_like(out_row)
    slots = slot_ref.shape[1] // 2
    counts = [jnp.int32(0), jnp.int32(0)]
    for j in range(rows):
        request = order_ref[me * rows + j]
        holder = div(request, rows)
        count = jnp.where(holder == 0, counts[0], counts[1])
        counts[0] = counts[0] + jnp.where(holder == 0, 1, 0)
        counts[1] = counts[1] + jnp.where(holder == 0, 0, 1)
        away = jnp.where(holder == me, 0, 1)
        here = place_of == j
        landed_row = jnp.where(here, holder * (tensor * group) + count, landed_row)
        residual_row = jnp.where(here, away * (steps * rows) + mod(request, rows), residual_row)
        slot = jnp.where(here, away * slots + adapter_ref[request], slot)
    landed_row = landed_row + step_of * half
    residual_row = residual_row + step_of * rows
    column = iota(mix_ref.shape, 1)
    kept = column - mod(column, tensor * group) + mod(column, group)
    mix_ref[...] = one_hot(kept == landed_row)
    slot_ref[...] = one_hot(iota(slot_ref.shape, 1) == slot).astype(f32)
    column = iota((steps * rows, steps * rows), 1)
    base_ref[...] = dot(
        one_hot(column == residual_row), residual_ref[...].reshape(steps * rows, features)
    ) + dot(
        one_hot(column + steps * rows == residual_row),
        other_residual_ref[...].reshape(steps * rows, features),
    )

    position = iota((table_blocks, block_size, width), 0) * block_size + iota(
        (table_blocks, block_size, width), 1
    )

    def store(j, carry):
        length = lengths_ref[order_ref[me * rows + j]]
        pltpu.make_async_copy(own_ref.at[pl.ds(0, table_blocks)], blocks_v.at[j], block_sem.at[j]).wait()
        values = blocks_v[j]
        blocks_v[j] = jnp.where(position < length, values, jnp.zeros_like(values))
        pltpu.make_async_copy(blocks_v.at[j], out_ref.at[j], out_sem).start()
        return carry

    lax.fori_loop(0, rows, store, 0)
    pltpu.make_async_copy(blocks_v, out_ref, out_sem).wait()


def place_call(order, lengths, table, adapters, own, other, residual, other_residual, tensor, slots):
    steps, rows, features = residual.shape
    _, block_size, width = own.shape
    smem = pl.BlockSpec(memory_space=pltpu.SMEM)
    vmem = pl.BlockSpec(memory_space=pltpu.VMEM)
    hbm = pl.BlockSpec(memory_space=pl.ANY)
    cache = (rows, table.shape[0], block_size, width)
    return pl.pallas_call(
        place_kernel,
        out_shape=(
            jax.ShapeDtypeStruct(cache, bf16),
            jax.ShapeDtypeStruct((steps * rows, features), f32),
            jax.ShapeDtypeStruct((steps * rows, tensor * steps * rows), bf16),
            jax.ShapeDtypeStruct((steps * rows, 2 * slots), f32),
        ),
        in_specs=[smem] * 4 + [hbm] * 2 + [vmem] * 2,
        out_specs=(hbm, vmem, vmem, vmem),
        scratch_shapes=[
            pltpu.VMEM(cache, bf16),
            pltpu.SemaphoreType.DMA((rows,)),
            pltpu.SemaphoreType.DMA,
        ],
        compiler_params=pltpu.CompilerParams(vmem_limit_bytes=VMEM_BYTES),
        name="place",
    )(order, lengths, table, adapters, own, other, residual, other_residual)


def finish_kernel(landed_ref, base_ref, mix_ref, slot_ref, up_ref, other_up_ref, out_ref):
    features = base_ref.shape[1]
    slots, rank = up_ref.shape[:2]
    sums = dot(mix_ref[...], landed_ref[...])
    shrink = sums[:, features : features + rank].astype(bf16).astype(f32)
    result = base_ref[...] + sums[:, :features]
    for side, up in enumerate((up_ref, other_up_ref)):
        wide = jnp.concatenate(
            [shrink * slot_ref[:, side * slots + n : side * slots + n + 1] for n in range(slots)],
            axis=1,
        ).astype(bf16)
        result = result + adapter_scale * dot(wide, up[...].reshape(slots * rank, features))
    out_ref[...] = result.astype(bf16).reshape(out_ref.shape)


def shards(
    queries,
    latest_key_value,
    residual,
    paged_cache_pool,
    adapter_down_weight,
    adapter_up_weight,
    output_weight,
    lengths,
    previous_block_table,
    request_order_after,
    request_adapter_index,
):
    steps, rows, features = queries.shape
    replicas = lax.axis_size("replica")
    tensor = lax.axis_size("tensor")
    blocks, _, block_size, width = paged_cache_pool.shape
    table_blocks = previous_block_table.shape[1]
    pool = paged_cache_pool.reshape(blocks, block_size, width)
    fresh = latest_key_value.reshape(steps, rows, width)
    swap = [(0, 1), (1, 0)]
    other_pool = lax.ppermute(pool, "replica", swap)
    other_residual = lax.ppermute(residual, "replica", swap)
    other_up = lax.ppermute(adapter_up_weight, "replica", swap)

    table = previous_block_table.T
    send = attend_call(
        request_order_after,
        lengths,
        table,
        request_adapter_index,
        queries,
        fresh,
        adapter_down_weight,
        pool,
        output_weight,
    )
    landed = lax.all_to_all(
        send.reshape((replicas * tensor,) + send.shape[2:]),
        ("replica", "tensor"),
        split_axis=0,
        concat_axis=0,
        tiled=True,
    ).reshape(send.shape)
    placed_cache, base, mix, slot = place_call(
        request_order_after,
        lengths,
        table,
        request_adapter_index,
        pool,
        other_pool,
        residual,
        other_residual,
        tensor,
        adapter_up_weight.shape[0],
    )
    vmem = pl.BlockSpec(memory_space=pltpu.VMEM)
    layer_out = pl.pallas_call(
        finish_kernel,
        out_shape=jax.ShapeDtypeStruct((steps, rows, features), bf16),
        in_specs=[vmem] * 6,
        out_specs=vmem,
        compiler_params=pltpu.CompilerParams(vmem_limit_bytes=VMEM_BYTES // 2),
        name="finish",
    )(landed.reshape(-1, landed.shape[-1]), base, mix, slot, adapter_up_weight, other_up)
    return (layer_out, placed_cache.reshape(rows, table_blocks, 1, block_size, width))


def solution(mesh):
    in_specs = (
        P(None, ("groups", "replica"), "tensor"),
        P(None, ("groups", "replica"), "tensor", None),
        P(None, ("groups", "replica"), "tensor"),
        P(("groups", "replica"), "tensor", None, None),
        P(("groups", "replica"), None, "tensor"),
        P(("groups", "replica"), None, "tensor"),
        P("tensor", None),
        P("groups"),
        P("groups", None),
        P("groups"),
        P("groups"),
    )
    out_specs = (
        P(None, ("groups", "replica"), "tensor"),
        P(("groups", "replica"), None, "tensor", None, None),
    )
    return jax.shard_map(shards, mesh=mesh, in_specs=in_specs, out_specs=out_specs, check_vma=False)
```

```python
import functools

import jax
import jax.numpy as jnp
from jax import lax
from jax.experimental import pallas as pl
from jax.experimental.pallas import tpu as pltpu
from jax.sharding import PartitionSpec as P

adapter_scale = 2.0
bf16 = jnp.bfloat16
f32 = jnp.float32
LANES = 128
QUAD = 4
VMEM_BYTES = 56 * 1024 * 1024
SMALL_BYTES = 8 * 1024 * 1024
MIDDLE_BYTES = 52 * 1024 * 1024


def iota(shape, dim):
    return lax.broadcasted_iota(jnp.int32, shape, dim)


def div(value, size):
    return value >> (size.bit_length() - 1) if size & (size - 1) == 0 else value // size


def mod(value, size):
    return value & (size - 1) if size & (size - 1) == 0 else value % size


def dot(a, b, contract=((1,), (0,))):
    return lax.dot_general(a, b, (contract, ((), ())), preferred_element_type=f32)


def one_hot(mask):
    return jnp.where(mask, 1.0, 0.0).astype(bf16)


def rank_rows(order_ref, found_ref, target_ref, holder, place, row_count, base):
    def step(j, count):
        request = order_ref[place * row_count + j]
        hit = div(request, row_count) == holder

        @pl.when(hit)
        def _():
            found_ref[base + count] = request - holder * row_count
            target_ref[base + count] = j

        return count + hit.astype(jnp.int32)

    lax.fori_loop(0, row_count, step, jnp.int32(0))


def weight_columns(weight_ref, weight_v, sems, partners):
    out_width = weight_v.shape[2]
    spans = weight_v.shape[0] // len(partners)
    here = lax.axis_index("tensor")
    copies = []
    for n, partner in enumerate(partners):
        for span in range(spans):
            start = pl.multiple_of((here ^ (span * QUAD + partner)) * out_width, out_width)
            slot = n * spans + span
            copies.append(
                pltpu.make_async_copy(
                    weight_ref.at[:, pl.ds(start, out_width)], weight_v.at[slot], sems.at[slot]
                )
            )
    return copies


def project(mixed, shrink, weight_copies, weight_v, message_refs):
    out_width = weight_v.shape[2]
    spans = weight_v.shape[0] // len(message_refs)
    for n, message_ref in enumerate(message_refs):
        message_ref[:, spans * out_width :] = shrink
        for span in range(spans):
            slot = n * spans + span
            weight_copies[slot].wait()
            part = dot(mixed, weight_v[slot]).astype(bf16)
            message_ref[:, span * out_width : (span + 1) * out_width] = part


def attend_kernel(
    order_ref,
    lengths_ref,
    table_ref,
    adapter_ref,
    queries_hbm,
    fresh_hbm,
    down_hbm,
    pool_ref,
    weight_ref,
    *rest,
    partners,
):
    message_refs, rest = rest[: len(partners)], rest[len(partners) :]
    (
        mixed_ref,
        shrink_ref,
        placed_ref,
        leaving_ref,
        queries_ref,
        fresh_ref,
        down_ref,
        pool_v,
        weight_v,
        scores_v,
        probs_v,
        attended_v,
        zero_v,
        found,
        target,
        small_sem,
        pool_sem,
        weight_sem,
        cache_sem,
    ) = rest
    steps, rows, features = queries_ref.shape
    blocks, block_size, width = pool_v.shape
    head = width // 2
    heads = features // head
    sh = steps * heads
    table_blocks = table_ref.shape[0]
    positions = table_blocks * block_size
    places = lengths_ref.shape[0] // rows
    half = rows // places
    slots, rank = down_ref.shape[:2]
    me = lax.axis_index("replica")
    first = me * rows

    small_copies = [
        pltpu.make_async_copy(source, target, small_sem.at[n])
        for n, (source, target) in enumerate(
            ((queries_hbm, queries_ref), (fresh_hbm, fresh_ref), (down_hbm, down_ref))
        )
    ]
    pool_copy = pltpu.make_async_copy(pool_ref, pool_v, pool_sem)
    weight_copies = weight_columns(weight_ref, weight_v, weight_sem, partners)
    small_copies[0].start()
    small_copies[1].start()
    pool_copy.start()
    small_copies[2].start()
    for copy in weight_copies[:2]:
        copy.start()

    for place in range(places):
        rank_rows(order_ref, found, target, me, me if place == 0 else 1 - me, rows, place * half)

    small_copies[0].wait()
    small_copies[1].wait()
    stacked = jnp.concatenate(
        [
            queries_ref[s, :, h * head : (h + 1) * head]
            for s in range(steps)
            for h in range(heads)
        ],
        axis=0,
    )
    total = rows * sh
    out_row, in_row = iota((total, total), 0), iota((total, total), 1)
    turn = one_hot((div(out_row, sh) == mod(in_row, rows)) & (mod(out_row, sh) == div(in_row, rows)))
    turned = dot(turn, stacked)
    query_rows = turned.astype(bf16)
    spread = one_hot(div(iota((total, rows), 0), sh) == iota((total, rows), 1))
    scale = head ** (-0.5)
    fresh_rows = [dot(spread, fresh_ref[s]) for s in range(steps)]
    step_of = div(mod(iota((total, 1), 0), sh), heads)
    fresh_scores = []
    for s in range(steps):
        value = jnp.sum(turned * fresh_rows[s][:, :head], axis=1, keepdims=True) * scale
        fresh_scores.append(jnp.where(step_of >= s, value, f32(-1e30)))

    pool_copy.wait()
    for copy in weight_copies[2:]:
        copy.start()

    def block_rows(row, lo):
        return jnp.concatenate(
            [pool_v[table_ref[b, first + row], :, lo : lo + head] for b in range(table_blocks)],
            axis=0,
        )

    zero_v[...] = jnp.zeros_like(zero_v)
    position = iota(zero_v.shape, 0)
    for row in range(rows):
        length = lengths_ref[first + row]
        full = div(length, block_size)

        @pl.when(full < table_blocks)
        def _(row=row, length=length, full=full):
            block = table_ref[full, first + row]
            kept = jnp.where(
                position < length - full * block_size, pool_v[block].astype(f32), 0.0
            )
            pool_v[block] = kept.astype(bf16)

    column = iota((sh, positions), 1)
    for row in range(rows):
        part = dot(query_rows[row * sh : (row + 1) * sh], block_rows(row, 0), ((1,), (1,)))
        part = jnp.where(column < lengths_ref[first + row], part * scale, f32(-1e30))
        scores_v[row * sh : (row + 1) * sh, :] = part

    scores = scores_v[...]
    top = jnp.max(scores, axis=1, keepdims=True)
    for value in fresh_scores:
        top = jnp.maximum(top, value)
    weights = jnp.exp(scores - top)
    fresh_weights = [jnp.exp(value - top) for value in fresh_scores]
    totals = jnp.sum(weights, axis=1, keepdims=True)
    for value in fresh_weights:
        totals = totals + value
    probs_v[...] = weights / totals

    for row in range(rows):
        span = slice(row * sh, (row + 1) * sh)
        attended_v[span, :] = dot(probs_v[span, :].astype(bf16), block_rows(row, head))
    attended = attended_v[...]
    for value, row in zip(fresh_weights, fresh_rows):
        share = (value / totals).astype(bf16).astype(f32)
        attended = attended + share * row[:, head:]
    attended = attended.astype(bf16)

    row_index = iota((places * steps * half, 1), 0)
    source = jnp.zeros_like(row_index)
    adapter = jnp.zeros_like(row_index)
    for place in range(places):
        for slot in range(half):
            local = found[place * half + slot]
            here = (div(row_index, steps * half) == place) & (mod(row_index, half) == slot)
            source = jnp.where(here, local, source)
            adapter = jnp.where(here, adapter_ref[first + local], adapter)
    step_index = div(mod(row_index, steps * half), half)
    columns = iota((places * steps * half, total), 1)
    pieces = []
    for h in range(heads):
        wanted = source * sh + step_index * heads + h
        pieces.append(dot(one_hot(columns == wanted), attended))
    mixed = jnp.concatenate(pieces, axis=1).astype(bf16)

    small_copies[2].wait()
    wide = dot(mixed, down_ref[...].reshape(slots * rank, features), ((1,), (1,)))
    shrink = jnp.zeros((places * steps * half, rank), f32)
    for slot in range(slots):
        shrink = shrink + jnp.where(
            adapter == slot, wide[:, slot * rank : (slot + 1) * rank], 0.0
        )
    shrink = jnp.concatenate(
        [shrink, jnp.zeros((places * steps * half, LANES - rank), f32)], axis=1
    ).astype(bf16)

    mixed_ref[...] = mixed
    shrink_ref[...] = shrink

    def write_cache(index, carry):
        local = found[index]
        length = lengths_ref[first + local]

        def write(row_ref, sem):
            for b in range(table_blocks):

                @pl.when(b * block_size < length)
                def _():
                    source = pool_v.at[table_ref[b, first + local]]
                    pltpu.make_async_copy(source, row_ref.at[b], sem).start()

                @pl.when(b * block_size >= length)
                def _():
                    pltpu.make_async_copy(zero_v, row_ref.at[b], sem).start()

        @pl.when(index < half)
        def _():
            write(placed_ref.at[target[index]], cache_sem.at[0])

        @pl.when(index >= half)
        def _():
            write(leaving_ref.at[index - half], cache_sem.at[1])

        return carry

    lax.fori_loop(0, rows, write_cache, 0)
    project(mixed, shrink, weight_copies, weight_v, message_refs)
    staying = placed_ref.at[pl.ds(0, half)]
    pltpu.make_async_copy(staying, staying, cache_sem.at[0]).wait()
    pltpu.make_async_copy(leaving_ref, leaving_ref, cache_sem.at[1]).wait()


def own_kernel(
    order_ref,
    adapter_ref,
    mixed_ref,
    shrink_ref,
    weight_ref,
    residual_ref,
    message_ref,
    stream_ref,
    mix_ref,
    slot_ref,
    weight_v,
    weight_sem,
):
    weight_copies = weight_columns(weight_ref, weight_v, weight_sem, (0,))
    for copy in weight_copies:
        copy.start()

    steps, rows, features = residual_ref.shape
    group = mix_ref.shape[0] // 2
    half = group // steps
    blocks = mix_ref.shape[1] // (2 * group)
    slots = slot_ref.shape[1] // 2
    me = lax.axis_index("replica")
    out_row = iota((steps * rows, 1), 0)
    step_of, place_of = div(out_row, rows), mod(out_row, rows)
    landed_row = jnp.zeros_like(out_row)
    slot = jnp.zeros_like(out_row)
    counts = [jnp.int32(0), jnp.int32(0)]
    for j in range(rows):
        request = order_ref[me * rows + j]
        away = jnp.where(div(request, rows) == me, 0, 1)
        count = jnp.where(away == 0, counts[0], counts[1])
        counts = [counts[0] + 1 - away, counts[1] + away]
        here = place_of == j
        landed_row = jnp.where(here, away * (blocks * group) + count, landed_row)
        slot = jnp.where(here, away * slots + adapter_ref[request], slot)
    landed_row = landed_row + step_of * half
    column = iota(mix_ref.shape, 1)
    kept = column - mod(column, blocks * group) + mod(column, group)
    mix_ref[...] = one_hot(kept == landed_row)
    slot_ref[...] = one_hot(iota(slot_ref.shape, 1) == slot).astype(f32)
    source = jnp.zeros_like(out_row)
    for side in range(2):
        place = me if side == 0 else 1 - me
        count = jnp.int32(0)
        for j in range(rows):
            request = order_ref[place * rows + j]
            hit = div(request, rows) == me
            index = jnp.where(hit, count, -1)
            here = (div(out_row, group) == side) & (mod(out_row, half) == index)
            source = jnp.where(here, mod(request, rows), source)
            count = count + hit.astype(jnp.int32)
    source = source + div(mod(out_row, group), half) * rows
    stream = dot(
        one_hot(iota((steps * rows, steps * rows), 1) == source),
        residual_ref[...].reshape(steps * rows, features),
    )
    stream_ref[:, :features] = stream.astype(bf16)
    stream_ref[:, features:] = jnp.zeros((steps * rows, LANES), bf16)

    project(mixed_ref[...], shrink_ref[...], weight_copies, weight_v, [message_ref])


def attend_call(order, lengths, table, adapters, queries, fresh, down, pool, weight, partners):
    steps, rows, features = queries.shape
    tensor = lax.axis_size("tensor")
    blocks, block_size, width = pool.shape
    positions = table.shape[0] * block_size
    score_rows = rows * steps * features // (width // 2)
    out_width = weight.shape[1] // tensor
    spans = tensor // QUAD
    message = (steps * rows, spans * out_width + LANES)
    cache = (table.shape[0], block_size, width)
    smem = pl.BlockSpec(memory_space=pltpu.SMEM)
    vmem = pl.BlockSpec(memory_space=pltpu.VMEM)
    hbm = pl.BlockSpec(memory_space=pl.ANY)
    return pl.pallas_call(
        functools.partial(attend_kernel, partners=partners),
        out_shape=[jax.ShapeDtypeStruct(message, bf16)] * len(partners)
        + [
            jax.ShapeDtypeStruct((steps * rows, features), bf16),
            jax.ShapeDtypeStruct((steps * rows, LANES), bf16),
            jax.ShapeDtypeStruct((rows,) + cache, bf16),
            jax.ShapeDtypeStruct((rows // lax.axis_size("replica"),) + cache, bf16),
        ],
        in_specs=[smem] * 4 + [hbm] * 5,
        out_specs=[vmem] * (len(partners) + 2) + [hbm] * 2,
        scratch_shapes=[
            pltpu.VMEM(queries.shape, bf16),
            pltpu.VMEM(fresh.shape, bf16),
            pltpu.VMEM(down.shape, bf16),
            pltpu.VMEM((blocks, block_size, width), bf16),
            pltpu.VMEM((len(partners) * spans, weight.shape[0], out_width), bf16),
            pltpu.VMEM((score_rows, positions), f32),
            pltpu.VMEM((score_rows, positions), f32),
            pltpu.VMEM((score_rows, width // 2), f32),
            pltpu.VMEM((block_size, width), bf16),
            pltpu.SMEM((rows,), jnp.int32),
            pltpu.SMEM((rows,), jnp.int32),
            pltpu.SemaphoreType.DMA((3,)),
            pltpu.SemaphoreType.DMA,
            pltpu.SemaphoreType.DMA((len(partners) * spans,)),
            pltpu.SemaphoreType.DMA((2,)),
        ],
        compiler_params=pltpu.CompilerParams(vmem_limit_bytes=VMEM_BYTES),
        name="attend",
    )(order, lengths, table, adapters, queries, fresh, down, pool, weight)


def own_call(order, adapters, mixed, shrink, weight, residual, slots):
    steps, rows, features = residual.shape
    tensor = lax.axis_size("tensor")
    out_width = weight.shape[1] // tensor
    spans = tensor // QUAD
    message = (mixed.shape[0], spans * out_width + LANES)
    smem = pl.BlockSpec(memory_space=pltpu.SMEM)
    vmem = pl.BlockSpec(memory_space=pltpu.VMEM)
    hbm = pl.BlockSpec(memory_space=pl.ANY)
    return pl.pallas_call(
        own_kernel,
        out_shape=(
            jax.ShapeDtypeStruct(message, bf16),
            jax.ShapeDtypeStruct((steps * rows, features + LANES), bf16),
            jax.ShapeDtypeStruct((steps * rows, (spans + 1) * steps * rows), bf16),
            jax.ShapeDtypeStruct((steps * rows, 2 * slots), f32),
        ),
        in_specs=[smem] * 2 + [vmem] * 2 + [hbm, vmem],
        out_specs=(vmem,) * 4,
        scratch_shapes=[
            pltpu.VMEM((spans, weight.shape[0], out_width), bf16),
            pltpu.SemaphoreType.DMA((spans,)),
        ],
        compiler_params=pltpu.CompilerParams(vmem_limit_bytes=MIDDLE_BYTES),
        cost_estimate=pl.CostEstimate(
            flops=2 * mixed.shape[0] * weight.shape[0] * spans * out_width,
            bytes_accessed=4 * weight.shape[0] * spans * out_width,
            transcendentals=0,
        ),
        name="own",
    )(order, adapters, mixed, shrink, weight, residual)


def merge_kernel(*refs, spans):
    stream_ref, messages, outs = refs[0], refs[1 : -2 * spans], refs[-2 * spans :]
    total = messages[0][...].astype(f32)
    for ref in messages[1:]:
        total = total + ref[...].astype(f32)
    total = total.astype(bf16)
    group = total.shape[0] // 2
    out_width = (total.shape[1] - LANES) // spans
    for side in range(2):
        span = slice(side * group, (side + 1) * group)
        for n in range(spans):
            ref = outs[side * spans + n]
            ref[:group, :out_width] = total[span, n * out_width : (n + 1) * out_width]
            ref[:group, out_width:] = total[span, spans * out_width :]
        outs[side * spans][group:] = stream_ref[span, :]


def merge_call(stream, messages, spans):
    rows, columns = messages[0].shape
    vmem = pl.BlockSpec(memory_space=pltpu.VMEM)
    width = (columns - LANES) // spans + LANES
    pieces = [
        jax.ShapeDtypeStruct((rows if n == 0 else rows // 2, width), bf16) for n in range(spans)
    ]
    pieces = pl.pallas_call(
        functools.partial(merge_kernel, spans=spans),
        out_shape=pieces * 2,
        in_specs=[vmem] * (1 + len(messages)),
        out_specs=[vmem] * (2 * spans),
        compiler_params=pltpu.CompilerParams(vmem_limit_bytes=SMALL_BYTES),
        name="merge",
    )(stream, *messages)
    return pieces[:spans], pieces[spans:]


def arrive_kernel(order_ref, arrived_ref, placed_in_ref, placed_ref, sem):
    rows = placed_ref.shape[0]
    me = lax.axis_index("replica")

    def step(j, count):
        hit = div(order_ref[me * rows + j], rows) != me

        @pl.when(hit)
        def _():
            pltpu.make_async_copy(arrived_ref.at[count], placed_ref.at[j], sem).start()

        return count + hit.astype(jnp.int32)

    lax.fori_loop(0, rows, step, jnp.int32(0))
    pltpu.make_async_copy(arrived_ref, arrived_ref, sem).wait()


def arrive_call(order, arrived, placed):
    hbm = pl.BlockSpec(memory_space=pl.ANY)
    return pl.pallas_call(
        arrive_kernel,
        out_shape=jax.ShapeDtypeStruct(placed.shape, bf16),
        in_specs=[
            pl.BlockSpec(memory_space=pltpu.SMEM),
            pl.BlockSpec(memory_space=pltpu.VMEM),
            hbm,
        ],
        out_specs=hbm,
        scratch_shapes=[pltpu.SemaphoreType.DMA],
        input_output_aliases={2: 0},
        compiler_params=pltpu.CompilerParams(vmem_limit_bytes=SMALL_BYTES),
        cost_estimate=pl.CostEstimate(
            flops=0, bytes_accessed=4 * arrived.size, transcendentals=0
        ),
        name="arrive",
    )(order, arrived, placed)


def finish_kernel(mix_ref, slot_ref, up_ref, other_up_ref, *rest):
    landed_refs, out_ref = rest[:-1], rest[-1]
    slots, rank, features = up_ref.shape
    sums = dot(mix_ref[...], jnp.concatenate([ref[...] for ref in landed_refs], axis=0))
    shrink = sums[:, features : features + rank].astype(bf16).astype(f32)
    result = sums[:, :features]
    for side, up in enumerate((up_ref, other_up_ref)):
        wide = jnp.concatenate(
            [shrink * slot_ref[:, side * slots + n : side * slots + n + 1] for n in range(slots)],
            axis=1,
        ).astype(bf16)
        result = result + adapter_scale * dot(wide, up[...].reshape(slots * rank, features))
    out_ref[...] = result.astype(bf16).reshape(out_ref.shape)


def shards(
    queries,
    latest_key_value,
    residual,
    paged_cache_pool,
    adapter_down_weight,
    adapter_up_weight,
    output_weight,
    lengths,
    previous_block_table,
    request_order_after,
    request_adapter_index,
):
    steps, rows, features = queries.shape
    replicas = lax.axis_size("replica")
    tensor = lax.axis_size("tensor")
    blocks, _, block_size, width = paged_cache_pool.shape
    table_blocks = previous_block_table.shape[1]
    pool = paged_cache_pool.reshape(blocks, block_size, width)
    fresh = latest_key_value.reshape(steps, rows, width)
    swap = [(0, 1), (1, 0)]
    other_up = lax.ppermute(adapter_up_weight, "replica", swap)

    table = previous_block_table.T
    *messages, mixed, shrink, placed, leaving = attend_call(
        request_order_after,
        lengths,
        table,
        request_adapter_index,
        queries,
        fresh,
        adapter_down_weight,
        pool,
        output_weight,
        (3, 2, 1),
    )
    spans = tensor // QUAD
    landed = []
    for partner, message in zip((3, 2, 1), messages):
        pairs = [(t, t ^ partner) for t in range(tensor)]
        landed.append(lax.ppermute(message, "tensor", pairs))
    own, stream, mix, slot = own_call(
        request_order_after,
        request_adapter_index,
        mixed,
        shrink,
        output_weight,
        residual,
        adapter_up_weight.shape[0],
    )
    arrived = lax.ppermute(leaving, "replica", swap)
    stays, leaves = merge_call(stream, [own] + landed, spans)

    def deliver(piece, span, away):
        pairs = [
            (r * tensor + t, (r ^ away) * tensor + (t ^ (span * QUAD)))
            for r in range(replicas)
            for t in range(tensor)
        ]
        return lax.ppermute(piece, ("replica", "tensor"), pairs)

    stays = [stays[0]] + [deliver(stays[n], n, 0) for n in range(1, spans)]
    leaves = [deliver(leaves[n], n, 1) for n in reversed(range(spans))][::-1]
    placed_cache = arrive_call(request_order_after, arrived, placed)
    placed_cache, mix = lax.optimization_barrier((placed_cache, mix))
    vmem = pl.BlockSpec(memory_space=pltpu.VMEM)
    layer_out = pl.pallas_call(
        finish_kernel,
        out_shape=jax.ShapeDtypeStruct((steps, rows, features), bf16),
        in_specs=[vmem] * (4 + 2 * spans),
        out_specs=vmem,
        compiler_params=pltpu.CompilerParams(vmem_limit_bytes=SMALL_BYTES),
        name="finish",
    )(mix, slot, adapter_up_weight, other_up, *stays, *leaves)
    return (layer_out, placed_cache.reshape(rows, table_blocks, 1, block_size, width))


def solution(mesh):
    in_specs = (
        P(None, ("groups", "replica"), "tensor"),
        P(None, ("groups", "replica"), "tensor", None),
        P(None, ("groups", "replica"), "tensor"),
        P(("groups", "replica"), "tensor", None, None),
        P(("groups", "replica"), None, "tensor"),
        P(("groups", "replica"), None, "tensor"),
        P("tensor", None),
        P("groups"),
        P("groups", None),
        P("groups"),
        P("groups"),
    )
    out_specs = (
        P(None, ("groups", "replica"), "tensor"),
        P(("groups", "replica"), None, "tensor", None, None),
    )
    return jax.shard_map(shards, mesh=mesh, in_specs=in_specs, out_specs=out_specs, check_vma=False)
```

```python
import functools

import jax
import jax.numpy as jnp
from jax import lax
from jax.experimental import pallas as pl
from jax.experimental.pallas import tpu as pltpu
from jax.sharding import PartitionSpec as P

adapter_scale = 2.0
bf16 = jnp.bfloat16
f32 = jnp.float32
LANES = 128
QUAD = 4
PARTNERS = ((3, 3), (2, 1), (1, 2))
ATTEND_FLOPS = 40_000_000_000
MERGE_FLOPS = 50_000_000_000
VMEM_BYTES = 56 * 1024 * 1024
SMALL_BYTES = 8 * 1024 * 1024


def iota(shape, dim):
    return lax.broadcasted_iota(jnp.int32, shape, dim)


def div(value, size):
    return value >> (size.bit_length() - 1) if size & (size - 1) == 0 else value // size


def mod(value, size):
    return value & (size - 1) if size & (size - 1) == 0 else value % size


def dot(a, b, contract=((1,), (0,))):
    return lax.dot_general(a, b, (contract, ((), ())), preferred_element_type=f32)


def one_hot(mask):
    return jnp.where(mask, 1.0, 0.0).astype(bf16)


def rank_rows(order_ref, found_ref, target_ref, holder, place, row_count, base):
    def step(j, count):
        request = order_ref[place * row_count + j]
        hit = div(request, row_count) == holder

        @pl.when(hit)
        def _():
            found_ref[base + count] = request - holder * row_count
            target_ref[base + count] = j

        return count + hit.astype(jnp.int32)

    lax.fori_loop(0, row_count, step, jnp.int32(0))


def project(mixed_ref, shrink_ref, weight_ref, message_ref, partner):
    out_width = weight_ref.shape[1] // lax.axis_size("tensor")
    spans = message_ref.shape[1] // out_width
    here = lax.axis_index("tensor")
    message_ref[:, spans * out_width :] = shrink_ref[...]
    for span in range(spans):
        start = pl.multiple_of((here ^ (span * QUAD + partner)) * out_width, out_width)
        part = dot(mixed_ref[...], weight_ref[:, pl.ds(start, out_width)])
        message_ref[:, span * out_width : (span + 1) * out_width] = part.astype(bf16)


def attend_kernel(
    order_ref,
    lengths_ref,
    table_ref,
    adapter_ref,
    queries_hbm,
    fresh_hbm,
    down_hbm,
    residual_hbm,
    pool_ref,
    mixed_ref,
    shrink_ref,
    pool_v,
    leaving_ref,
    stream_ref,
    mix_ref,
    slot_ref,
    queries_ref,
    fresh_ref,
    down_ref,
    residual_ref,
    scores_v,
    probs_v,
    attended_v,
    found,
    target,
    small_sem,
    pool_sem,
):
    steps, rows, features = queries_ref.shape
    blocks, block_size, width = pool_v.shape
    head = width // 2
    heads = features // head
    sh = steps * heads
    table_blocks = table_ref.shape[0]
    positions = table_blocks * block_size
    places = lengths_ref.shape[0] // rows
    half = rows // places
    slots, rank = down_ref.shape[:2]
    me = lax.axis_index("replica")
    first = me * rows

    small_copies = [
        pltpu.make_async_copy(source, target, small_sem.at[n])
        for n, (source, target) in enumerate(
            (
                (queries_hbm, queries_ref),
                (fresh_hbm, fresh_ref),
                (down_hbm, down_ref),
                (residual_hbm, residual_ref),
            )
        )
    ]
    pool_copy = pltpu.make_async_copy(pool_ref, pool_v, pool_sem)
    small_copies[0].start()
    small_copies[1].start()
    pool_copy.start()
    small_copies[2].start()
    small_copies[3].start()

    for place in range(places):
        rank_rows(order_ref, found, target, me, me if place == 0 else 1 - me, rows, place * half)

    small_copies[0].wait()
    small_copies[1].wait()
    stacked = jnp.concatenate(
        [
            queries_ref[s, :, h * head : (h + 1) * head]
            for s in range(steps)
            for h in range(heads)
        ],
        axis=0,
    )
    total = rows * sh
    out_row, in_row = iota((total, total), 0), iota((total, total), 1)
    turn = one_hot((div(out_row, sh) == mod(in_row, rows)) & (mod(out_row, sh) == div(in_row, rows)))
    turned = dot(turn, stacked)
    query_rows = turned.astype(bf16)
    spread = one_hot(div(iota((total, rows), 0), sh) == iota((total, rows), 1))
    scale = head ** (-0.5)
    fresh_rows = [dot(spread, fresh_ref[s]) for s in range(steps)]
    step_of = div(mod(iota((total, 1), 0), sh), heads)
    fresh_scores = []
    for s in range(steps):
        value = jnp.sum(turned * fresh_rows[s][:, :head], axis=1, keepdims=True) * scale
        fresh_scores.append(jnp.where(step_of >= s, value, f32(-1e30)))

    pool_copy.wait()

    def block_rows(row, lo):
        return jnp.concatenate(
            [pool_v[table_ref[b, first + row], :, lo : lo + head] for b in range(table_blocks)],
            axis=0,
        )

    position = iota((block_size, width), 0)
    for row in range(rows):
        length = lengths_ref[first + row]
        full = div(length, block_size)

        @pl.when(full < table_blocks)
        def _(row=row, length=length, full=full):
            block = table_ref[full, first + row]
            kept = jnp.where(
                position < length - full * block_size, pool_v[block].astype(f32), 0.0
            )
            pool_v[block] = kept.astype(bf16)

    column = iota((sh, positions), 1)
    for row in range(rows):
        part = dot(query_rows[row * sh : (row + 1) * sh], block_rows(row, 0), ((1,), (1,)))
        part = jnp.where(column < lengths_ref[first + row], part * scale, f32(-1e30))
        scores_v[row * sh : (row + 1) * sh, :] = part

    scores = scores_v[...]
    top = jnp.max(scores, axis=1, keepdims=True)
    for value in fresh_scores:
        top = jnp.maximum(top, value)
    weights = jnp.exp(scores - top)
    fresh_weights = [jnp.exp(value - top) for value in fresh_scores]
    totals = jnp.sum(weights, axis=1, keepdims=True)
    for value in fresh_weights:
        totals = totals + value
    probs_v[...] = weights / totals

    for row in range(rows):
        span = slice(row * sh, (row + 1) * sh)
        attended_v[span, :] = dot(probs_v[span, :].astype(bf16), block_rows(row, head))
    attended = attended_v[...]
    for value, row in zip(fresh_weights, fresh_rows):
        share = (value / totals).astype(bf16).astype(f32)
        attended = attended + share * row[:, head:]
    attended = attended.astype(bf16)

    row_index = iota((places * steps * half, 1), 0)
    source = jnp.zeros_like(row_index)
    adapter = jnp.zeros_like(row_index)
    for place in range(places):
        for slot in range(half):
            local = found[place * half + slot]
            here = (div(row_index, steps * half) == place) & (mod(row_index, half) == slot)
            source = jnp.where(here, local, source)
            adapter = jnp.where(here, adapter_ref[first + local], adapter)
    step_index = div(mod(row_index, steps * half), half)
    columns = iota((places * steps * half, total), 1)
    pieces = []
    for h in range(heads):
        wanted = source * sh + step_index * heads + h
        pieces.append(dot(one_hot(columns == wanted), attended))
    mixed = jnp.concatenate(pieces, axis=1).astype(bf16)

    small_copies[2].wait()
    wide = dot(mixed, down_ref[...].reshape(slots * rank, features), ((1,), (1,)))
    shrink = jnp.zeros((places * steps * half, rank), f32)
    for slot in range(slots):
        shrink = shrink + jnp.where(
            adapter == slot, wide[:, slot * rank : (slot + 1) * rank], 0.0
        )
    shrink = jnp.concatenate(
        [shrink, jnp.zeros((places * steps * half, LANES - rank), f32)], axis=1
    ).astype(bf16)

    mixed_ref[...] = mixed
    shrink_ref[...] = shrink

    def copy_leaving(index, carry):
        request = first + found[half + index]
        length = lengths_ref[request]
        for b in range(table_blocks):

            @pl.when(b * block_size < length)
            def _():
                leaving_ref[index, b] = pool_v[table_ref[b, request]]

            @pl.when(b * block_size >= length)
            def _():
                leaving_ref[index, b] = jnp.zeros((block_size, width), bf16)

        return carry

    lax.fori_loop(0, half, copy_leaving, 0)

    small_copies[3].wait()
    wanted = step_index * rows + source
    stream = dot(
        one_hot(iota((steps * rows, steps * rows), 1) == wanted),
        residual_ref[...].reshape(steps * rows, features),
    )
    stream_ref[:, :features] = stream.astype(bf16)
    stream_ref[:, features:] = jnp.zeros((steps * rows, LANES), bf16)

    group = steps * half
    landed_blocks = mix_ref.shape[1] // (places * group)
    out_row = iota((steps * rows, 1), 0)
    step_of, place_of = div(out_row, rows), mod(out_row, rows)
    landed_row = jnp.zeros_like(out_row)
    slot_of = jnp.zeros_like(out_row)
    counts = [jnp.int32(0), jnp.int32(0)]
    for j in range(rows):
        request = order_ref[first + j]
        away = jnp.where(div(request, rows) == me, 0, 1)
        count = jnp.where(away == 0, counts[0], counts[1])
        counts = [counts[0] + 1 - away, counts[1] + away]
        here = place_of == j
        landed_row = jnp.where(here, away * (landed_blocks * group) + count, landed_row)
        slot_of = jnp.where(here, away * slots + adapter_ref[request], slot_of)
    landed_row = landed_row + step_of * half
    column = iota(mix_ref.shape, 1)
    kept = column - mod(column, landed_blocks * group) + mod(column, group)
    mix_ref[...] = one_hot(kept == landed_row)
    slot_ref[...] = one_hot(iota(slot_ref.shape, 1) == slot_of).astype(f32)


def message_kernel(mixed_ref, shrink_ref, weight_ref, message_ref, *, partners):
    partner = jnp.where(lax.axis_index("replica") == 0, partners[0], partners[1])
    project(mixed_ref, shrink_ref, weight_ref, message_ref, partner)


def stay_kernel(order_ref, lengths_ref, table_ref, pool_v, placed_ref, zero_v, sem):
    rows, table_blocks, block_size, _ = placed_ref.shape
    me = lax.axis_index("replica")
    zero_v[...] = jnp.zeros_like(zero_v)

    def step(j, carry):
        request = order_ref[me * rows + j]
        length = lengths_ref[request]

        @pl.when(div(request, rows) == me)
        def _():
            for b in range(table_blocks):
                target = placed_ref.at[j, b]

                @pl.when(b * block_size < length)
                def _():
                    source = pool_v.at[table_ref[b, request]]
                    pltpu.make_async_copy(source, target, sem).start()

                @pl.when(b * block_size >= length)
                def _():
                    pltpu.make_async_copy(zero_v, target, sem).start()

        return carry

    lax.fori_loop(0, rows, step, 0)
    staying = placed_ref.at[pl.ds(0, rows // 2)]
    pltpu.make_async_copy(staying, staying, sem).wait()


def in_hbm(value):
    return pltpu.with_memory_space_constraint(value, pltpu.HBM)


def attend_call(order, lengths, table, adapters, queries, fresh, down, residual, pool):
    steps, rows, features = queries.shape
    blocks, block_size, width = pool.shape
    table_blocks = table.shape[0]
    positions = table_blocks * block_size
    score_rows = rows * steps * features // (width // 2)
    spans = lax.axis_size("tensor") // QUAD
    smem = pl.BlockSpec(memory_space=pltpu.SMEM)
    vmem = pl.BlockSpec(memory_space=pltpu.VMEM)
    hbm = pl.BlockSpec(memory_space=pl.ANY)
    return pl.pallas_call(
        attend_kernel,
        out_shape=(
            pltpu.VMEM((steps * rows, features), bf16),
            pltpu.VMEM((steps * rows, LANES), bf16),
            pltpu.VMEM(pool.shape, bf16),
            pltpu.VMEM((rows // 2, table_blocks, block_size, width), bf16),
            pltpu.VMEM((steps * rows, features + LANES), bf16),
            pltpu.VMEM((steps * rows, (spans + 1) * steps * rows), bf16),
            pltpu.VMEM((steps * rows, 2 * down.shape[0]), f32),
        ),
        in_specs=[smem] * 4 + [hbm] * 5,
        out_specs=(vmem,) * 7,
        scratch_shapes=[
            pltpu.VMEM(queries.shape, bf16),
            pltpu.VMEM(fresh.shape, bf16),
            pltpu.VMEM(down.shape, bf16),
            pltpu.VMEM(residual.shape, bf16),
            pltpu.VMEM((score_rows, positions), f32),
            pltpu.VMEM((score_rows, positions), f32),
            pltpu.VMEM((score_rows, width // 2), f32),
            pltpu.SMEM((rows,), jnp.int32),
            pltpu.SMEM((rows,), jnp.int32),
            pltpu.SemaphoreType.DMA((4,)),
            pltpu.SemaphoreType.DMA,
        ],
        compiler_params=pltpu.CompilerParams(vmem_limit_bytes=2 * SMALL_BYTES),
        cost_estimate=pl.CostEstimate(
            flops=ATTEND_FLOPS, bytes_accessed=4 * pool.size, transcendentals=0
        ),
        name="attend",
    )(*(in_hbm(x) for x in (order, lengths, table, adapters, queries, fresh, down, residual, pool)))


def message_call(mixed, shrink, weight, partners):
    tensor = lax.axis_size("tensor")
    spans = tensor // QUAD
    columns = spans * weight.shape[1] // tensor
    vmem = pl.BlockSpec(memory_space=pltpu.VMEM)
    return pl.pallas_call(
        functools.partial(message_kernel, partners=partners),
        out_shape=pltpu.VMEM((mixed.shape[0], columns + LANES), bf16),
        in_specs=[vmem] * 3,
        out_specs=vmem,
        compiler_params=pltpu.CompilerParams(vmem_limit_bytes=SMALL_BYTES),
        name="message",
    )(mixed, shrink, weight)


def stay_call(order, lengths, table, pool, rows):
    smem = pl.BlockSpec(memory_space=pltpu.SMEM)
    vmem = pl.BlockSpec(memory_space=pltpu.VMEM)
    return pl.pallas_call(
        stay_kernel,
        out_shape=jax.ShapeDtypeStruct((rows, table.shape[0]) + pool.shape[1:], bf16),
        in_specs=[smem] * 3 + [vmem],
        out_specs=pl.BlockSpec(memory_space=pl.ANY),
        scratch_shapes=[pltpu.VMEM(pool.shape[1:], bf16), pltpu.SemaphoreType.DMA],
        compiler_params=pltpu.CompilerParams(vmem_limit_bytes=SMALL_BYTES),
        cost_estimate=pl.CostEstimate(flops=0, bytes_accessed=2 * pool.size, transcendentals=0),
        name="stay",
    )(order, lengths, table, pool)


def merge_kernel(*refs, spans):
    stream_ref, messages, outs = refs[0], refs[1 : -2 * spans], refs[-2 * spans :]
    total = messages[0][...].astype(f32)
    for ref in messages[1:]:
        total = total + ref[...].astype(f32)
    total = total.astype(bf16)
    group = total.shape[0] // 2
    out_width = (total.shape[1] - LANES) // spans
    for side in range(2):
        span = slice(side * group, (side + 1) * group)
        for n in range(spans):
            ref = outs[side * spans + n]
            ref[:group, :out_width] = total[span, n * out_width : (n + 1) * out_width]
            ref[:group, out_width:] = total[span, spans * out_width :]
        outs[side * spans][group:] = stream_ref[span, :]


def merge_call(stream, messages, spans):
    rows, columns = messages[0].shape
    vmem = pl.BlockSpec(memory_space=pltpu.VMEM)
    width = (columns - LANES) // spans + LANES
    pieces = [
        jax.ShapeDtypeStruct((rows if n == 0 else rows // 2, width), bf16) for n in range(spans)
    ]
    pieces = pl.pallas_call(
        functools.partial(merge_kernel, spans=spans),
        out_shape=pieces * 2,
        in_specs=[vmem] * (1 + len(messages)),
        out_specs=[vmem] * (2 * spans),
        compiler_params=pltpu.CompilerParams(vmem_limit_bytes=SMALL_BYTES),
        cost_estimate=pl.CostEstimate(flops=MERGE_FLOPS, bytes_accessed=0, transcendentals=0),
        name="merge",
    )(stream, *messages)
    return pieces[:spans], pieces[spans:]


def arrive_kernel(order_ref, arrived_ref, placed_in_ref, placed_ref, sem):
    rows = placed_ref.shape[0]
    me = lax.axis_index("replica")

    def step(j, count):
        hit = div(order_ref[me * rows + j], rows) != me

        @pl.when(hit)
        def _():
            pltpu.make_async_copy(arrived_ref.at[count], placed_ref.at[j], sem).start()

        return count + hit.astype(jnp.int32)

    lax.fori_loop(0, rows, step, jnp.int32(0))
    pltpu.make_async_copy(arrived_ref, arrived_ref, sem).wait()


def arrive_call(order, arrived, placed):
    hbm = pl.BlockSpec(memory_space=pl.ANY)
    return pl.pallas_call(
        arrive_kernel,
        out_shape=jax.ShapeDtypeStruct(placed.shape, bf16),
        in_specs=[
            pl.BlockSpec(memory_space=pltpu.SMEM),
            pl.BlockSpec(memory_space=pltpu.VMEM),
            hbm,
        ],
        out_specs=hbm,
        scratch_shapes=[pltpu.SemaphoreType.DMA],
        input_output_aliases={2: 0},
        compiler_params=pltpu.CompilerParams(vmem_limit_bytes=SMALL_BYTES),
        cost_estimate=pl.CostEstimate(
            flops=0, bytes_accessed=4 * arrived.size, transcendentals=0
        ),
        name="arrive",
    )(order, arrived, placed)


def finish_kernel(mix_ref, slot_ref, up_ref, other_up_ref, *rest):
    landed_refs, out_ref = rest[:-1], rest[-1]
    slots, rank, features = up_ref.shape
    sums = dot(mix_ref[...], jnp.concatenate([ref[...] for ref in landed_refs], axis=0))
    shrink = sums[:, features : features + rank].astype(bf16).astype(f32)
    result = sums[:, :features]
    for side, up in enumerate((up_ref, other_up_ref)):
        wide = jnp.concatenate(
            [shrink * slot_ref[:, side * slots + n : side * slots + n + 1] for n in range(slots)],
            axis=1,
        ).astype(bf16)
        result = result + adapter_scale * dot(wide, up[...].reshape(slots * rank, features))
    out_ref[...] = result.astype(bf16).reshape(out_ref.shape)


def shards(
    queries,
    latest_key_value,
    residual,
    paged_cache_pool,
    adapter_down_weight,
    adapter_up_weight,
    output_weight,
    lengths,
    previous_block_table,
    request_order_after,
    request_adapter_index,
):
    steps, rows, features = queries.shape
    replicas = lax.axis_size("replica")
    tensor = lax.axis_size("tensor")
    blocks, _, block_size, width = paged_cache_pool.shape
    table_blocks = previous_block_table.shape[1]
    pool = paged_cache_pool.reshape(blocks, block_size, width)
    fresh = latest_key_value.reshape(steps, rows, width)
    swap = [(0, 1), (1, 0)]
    other_up = lax.ppermute(adapter_up_weight, "replica", swap)

    table = previous_block_table.T
    integers = (request_order_after, lengths, table, request_adapter_index)
    mixed, shrink, pool, leaving, stream, mix, slot = attend_call(
        *integers, queries, fresh, adapter_down_weight, residual, pool
    )
    spans = tensor // QUAD
    landed = []
    for partners in PARTNERS:
        message = message_call(mixed, shrink, output_weight, partners)
        pairs = [
            (r * tensor + t, r * tensor + (t ^ partners[r]))
            for r in range(replicas)
            for t in range(tensor)
        ]
        landed.append(lax.ppermute(message, ("replica", "tensor"), pairs))
    own = message_call(mixed, shrink, output_weight, (0, 0))
    placed = stay_call(*integers[:3], pool, rows)
    arrived = lax.ppermute(leaving, "replica", swap)
    stays, leaves = merge_call(stream, [own] + landed, spans)

    def deliver(piece, span, away):
        pairs = [
            (r * tensor + t, (r ^ away) * tensor + (t ^ (span * QUAD)))
            for r in range(replicas)
            for t in range(tensor)
        ]
        return lax.ppermute(piece, ("replica", "tensor"), pairs)

    stays = [stays[0]] + [deliver(stays[n], n, 0) for n in range(1, spans)]
    leaves = [deliver(leaves[n], n, 1) for n in reversed(range(spans))][::-1]
    placed_cache = arrive_call(request_order_after, arrived, placed)
    placed_cache, mix = lax.optimization_barrier((placed_cache, mix))
    vmem = pl.BlockSpec(memory_space=pltpu.VMEM)
    layer_out = pl.pallas_call(
        finish_kernel,
        out_shape=jax.ShapeDtypeStruct((steps, rows, features), bf16),
        in_specs=[vmem] * (4 + 2 * spans),
        out_specs=vmem,
        compiler_params=pltpu.CompilerParams(vmem_limit_bytes=SMALL_BYTES),
        name="finish",
    )(mix, slot, adapter_up_weight, other_up, *stays, *leaves)
    return (layer_out, placed_cache.reshape(rows, table_blocks, 1, block_size, width))


def solution(mesh):
    in_specs = (
        P(None, ("groups", "replica"), "tensor"),
        P(None, ("groups", "replica"), "tensor", None),
        P(None, ("groups", "replica"), "tensor"),
        P(("groups", "replica"), "tensor", None, None),
        P(("groups", "replica"), None, "tensor"),
        P(("groups", "replica"), None, "tensor"),
        P("tensor", None),
        P("groups"),
        P("groups", None),
        P("groups"),
        P("groups"),
    )
    out_specs = (
        P(None, ("groups", "replica"), "tensor"),
        P(("groups", "replica"), None, "tensor", None, None),
    )
    return jax.shard_map(shards, mesh=mesh, in_specs=in_specs, out_specs=out_specs, check_vma=False)
```

```python
import functools

import jax
import jax.numpy as jnp
from jax import lax
from jax.experimental import pallas as pl
from jax.experimental.pallas import tpu as pltpu
from jax.sharding import PartitionSpec as P

adapter_scale = 2.0
bf16 = jnp.bfloat16
f32 = jnp.float32
LANES = 128
QUAD = 4
PARTNERS = ((3, 3), (2, 2), (1, 1))
ATTEND_FLOPS = 40_000_000_000
PREPARE_FLOPS = 2_000_000_000
MERGE_FLOPS = 50_000_000_000
VMEM_BYTES = 56 * 1024 * 1024
SMALL_BYTES = 8 * 1024 * 1024


def iota(shape, dim):
    return lax.broadcasted_iota(jnp.int32, shape, dim)


def div(value, size):
    return value >> (size.bit_length() - 1) if size & (size - 1) == 0 else value // size


def mod(value, size):
    return value & (size - 1) if size & (size - 1) == 0 else value % size


def dot(a, b, contract=((1,), (0,))):
    return lax.dot_general(a, b, (contract, ((), ())), preferred_element_type=f32)


def one_hot(mask):
    return jnp.where(mask, 1.0, 0.0).astype(bf16)


def rank_rows(order_ref, found_ref, target_ref, holder, place, row_count, base):
    def step(j, count):
        request = order_ref[place * row_count + j]
        hit = div(request, row_count) == holder

        @pl.when(hit)
        def _():
            found_ref[base + count] = request - holder * row_count
            target_ref[base + count] = j

        return count + hit.astype(jnp.int32)

    lax.fori_loop(0, row_count, step, jnp.int32(0))


def attend_kernel(
    order_ref,
    lengths_ref,
    table_ref,
    adapter_ref,
    queries_hbm,
    fresh_hbm,
    down_hbm,
    residual_hbm,
    pool_ref,
    stay_ref,
    leave_ref,
    pool_v,
    queries_ref,
    fresh_ref,
    down_ref,
    residual_ref,
    scores_v,
    probs_v,
    attended_v,
    found,
    target,
    small_sem,
    pool_sem,
):
    steps, rows, features = queries_ref.shape
    blocks, block_size, width = pool_v.shape
    head = width // 2
    heads = features // head
    sh = steps * heads
    table_blocks = table_ref.shape[0]
    positions = table_blocks * block_size
    places = lengths_ref.shape[0] // rows
    half = rows // places
    slots, rank = down_ref.shape[:2]
    me = lax.axis_index("replica")
    first = me * rows

    small_copies = [
        pltpu.make_async_copy(source, target, small_sem.at[n])
        for n, (source, target) in enumerate(
            (
                (queries_hbm, queries_ref),
                (fresh_hbm, fresh_ref),
                (down_hbm, down_ref),
                (residual_hbm, residual_ref),
            )
        )
    ]
    pool_copy = pltpu.make_async_copy(pool_ref, pool_v, pool_sem)
    small_copies[0].start()
    small_copies[1].start()
    pool_copy.start()
    small_copies[2].start()
    small_copies[3].start()

    for place in range(places):
        rank_rows(order_ref, found, target, me, me if place == 0 else 1 - me, rows, place * half)

    small_copies[0].wait()
    small_copies[1].wait()
    stacked = jnp.concatenate(
        [
            queries_ref[s, :, h * head : (h + 1) * head]
            for s in range(steps)
            for h in range(heads)
        ],
        axis=0,
    )
    total = rows * sh
    out_row, in_row = iota((total, total), 0), iota((total, total), 1)
    turn = one_hot((div(out_row, sh) == mod(in_row, rows)) & (mod(out_row, sh) == div(in_row, rows)))
    turned = dot(turn, stacked)
    query_rows = turned.astype(bf16)
    spread = one_hot(div(iota((total, rows), 0), sh) == iota((total, rows), 1))
    scale = head ** (-0.5)
    fresh_rows = [dot(spread, fresh_ref[s]) for s in range(steps)]
    step_of = div(mod(iota((total, 1), 0), sh), heads)
    fresh_scores = []
    for s in range(steps):
        value = jnp.sum(turned * fresh_rows[s][:, :head], axis=1, keepdims=True) * scale
        fresh_scores.append(jnp.where(step_of >= s, value, f32(-1e30)))

    pool_copy.wait()

    def block_rows(row, lo):
        return jnp.concatenate(
            [pool_v[table_ref[b, first + row], :, lo : lo + head] for b in range(table_blocks)],
            axis=0,
        )

    position = iota((block_size, width), 0)
    for row in range(rows):
        length = lengths_ref[first + row]
        full = div(length, block_size)

        @pl.when(full < table_blocks)
        def _(row=row, length=length, full=full):
            block = table_ref[full, first + row]
            kept = jnp.where(
                position < length - full * block_size, pool_v[block].astype(f32), 0.0
            )
            pool_v[block] = kept.astype(bf16)

    column = iota((sh, positions), 1)
    for row in range(rows):
        part = dot(query_rows[row * sh : (row + 1) * sh], block_rows(row, 0), ((1,), (1,)))
        part = jnp.where(column < lengths_ref[first + row], part * scale, f32(-1e30))
        scores_v[row * sh : (row + 1) * sh, :] = part

    scores = scores_v[...]
    top = jnp.max(scores, axis=1, keepdims=True)
    for value in fresh_scores:
        top = jnp.maximum(top, value)
    weights = jnp.exp(scores - top)
    fresh_weights = [jnp.exp(value - top) for value in fresh_scores]
    totals = jnp.sum(weights, axis=1, keepdims=True)
    for value in fresh_weights:
        totals = totals + value
    probs_v[...] = weights / totals

    for row in range(rows):
        span = slice(row * sh, (row + 1) * sh)
        attended_v[span, :] = dot(probs_v[span, :].astype(bf16), block_rows(row, head))
    attended = attended_v[...]
    for value, row in zip(fresh_weights, fresh_rows):
        share = (value / totals).astype(bf16).astype(f32)
        attended = attended + share * row[:, head:]
    attended = attended.astype(bf16)

    row_index = iota((places * steps * half, 1), 0)
    source = jnp.zeros_like(row_index)
    adapter = jnp.zeros_like(row_index)
    for place in range(places):
        for slot in range(half):
            local = found[place * half + slot]
            here = (div(row_index, steps * half) == place) & (mod(row_index, half) == slot)
            source = jnp.where(here, local, source)
            adapter = jnp.where(here, adapter_ref[first + local], adapter)
    step_index = div(mod(row_index, steps * half), half)
    columns = iota((places * steps * half, total), 1)
    pieces = []
    for h in range(heads):
        wanted = source * sh + step_index * heads + h
        pieces.append(dot(one_hot(columns == wanted), attended))
    mixed = jnp.concatenate(pieces, axis=1).astype(bf16)

    small_copies[2].wait()
    wide = dot(mixed, down_ref[...].reshape(slots * rank, features), ((1,), (1,)))
    shrink = jnp.zeros((places * steps * half, rank), f32)
    for slot in range(slots):
        shrink = shrink + jnp.where(
            adapter == slot, wide[:, slot * rank : (slot + 1) * rank], 0.0
        )
    shrink = jnp.concatenate(
        [shrink, jnp.zeros((places * steps * half, LANES - rank), f32)], axis=1
    ).astype(bf16)

    small_copies[3].wait()
    wanted = step_index * rows + source
    stream = dot(
        one_hot(iota((steps * rows, steps * rows), 1) == wanted),
        residual_ref[...].reshape(steps * rows, features),
    ).astype(bf16)
    group = steps * half
    for place, ref in enumerate((stay_ref, leave_ref)):
        span = slice(place * group, (place + 1) * group)
        ref[:, :features] = mixed[span]
        ref[:, features : features + LANES] = shrink[span]
        ref[:, features + LANES :] = stream[span]


def prepare_kernel(
    order_ref,
    lengths_ref,
    table_ref,
    adapter_ref,
    pool_v,
    leaving_ref,
    turn_ref,
    slot_ref,
):
    half, table_blocks, block_size, width = leaving_ref.shape
    rows = 2 * half
    group = turn_ref.shape[0] // 2
    me = lax.axis_index("replica")

    def copy_leaving(j, count):
        request = order_ref[(1 - me) * rows + j]
        hit = div(request, rows) == me

        @pl.when(hit)
        def _():
            length = lengths_ref[request]
            for b in range(table_blocks):

                @pl.when(b * block_size < length)
                def _():
                    leaving_ref[count, b] = pool_v[table_ref[b, request]]

                @pl.when(b * block_size >= length)
                def _():
                    leaving_ref[count, b] = jnp.zeros((block_size, width), bf16)

        return count + hit.astype(jnp.int32)

    lax.fori_loop(0, rows, copy_leaving, jnp.int32(0))

    row = iota((2 * group, 1), 0)
    step_of, place_of = div(row, rows), mod(row, rows)
    side_of, rank_of = div(row, group), mod(row, half)
    wanted = jnp.zeros_like(row)
    adapter = jnp.zeros_like(row)
    counts = [jnp.int32(0), jnp.int32(0)]
    for j in range(rows):
        request = order_ref[me * rows + j]
        away = jnp.where(div(request, rows) == me, 0, 1)
        count = jnp.where(away == 0, counts[0], counts[1])
        counts = [counts[0] + 1 - away, counts[1] + away]
        wanted = jnp.where(place_of == j, away * group + count, wanted)
        here = (side_of == away) & (rank_of == count)
        adapter = jnp.where(here, adapter_ref[request], adapter)
    wanted = wanted + step_of * half
    turn_ref[...] = one_hot(iota(turn_ref.shape, 1) == wanted)
    slot_ref[...] = one_hot(iota(slot_ref.shape, 1) == adapter).astype(f32)


def message_kernel(stay_ref, arrived_ref, weight_ref, message_ref, *, partners):
    out_width = weight_ref.shape[1] // lax.axis_size("tensor")
    features = weight_ref.shape[0]
    spans = message_ref.shape[1] // out_width
    here = lax.axis_index("tensor")
    partner = jnp.where(lax.axis_index("replica") == 0, partners[0], partners[1])
    mixed = jnp.concatenate([stay_ref[:, :features], arrived_ref[:, :features]], axis=0)
    group = stay_ref.shape[0]
    for side, ref in enumerate((stay_ref, arrived_ref)):
        shrink = ref[:, features : features + LANES].astype(message_ref.dtype)
        message_ref[side * group : (side + 1) * group, spans * out_width :] = shrink
    for span in range(spans):
        start = pl.multiple_of((here ^ (span * QUAD + partner)) * out_width, out_width)
        part = dot(mixed, weight_ref[:, pl.ds(start, out_width)])
        message_ref[:, span * out_width : (span + 1) * out_width] = part.astype(message_ref.dtype)


def place_kernel(order_ref, lengths_ref, table_ref, pool_v, arrived_ref, placed_ref, zero_v, sem):
    rows, table_blocks, block_size, _ = placed_ref.shape
    me = lax.axis_index("replica")
    zero_v[...] = jnp.zeros_like(zero_v)

    def step(j, count):
        request = order_ref[me * rows + j]
        length = lengths_ref[request]
        stayed = div(request, rows) == me

        @pl.when(jnp.logical_not(stayed))
        def _():
            pltpu.make_async_copy(arrived_ref.at[count], placed_ref.at[j], sem).start()

        @pl.when(stayed)
        def _():
            for b in range(table_blocks):
                target = placed_ref.at[j, b]

                @pl.when(b * block_size < length)
                def _():
                    source = pool_v.at[table_ref[b, request]]
                    pltpu.make_async_copy(source, target, sem).start()

                @pl.when(b * block_size >= length)
                def _():
                    pltpu.make_async_copy(zero_v, target, sem).start()

        return count + 1 - stayed.astype(jnp.int32)

    lax.fori_loop(0, rows, step, jnp.int32(0))
    pltpu.make_async_copy(placed_ref, placed_ref, sem).wait()


def in_hbm(value):
    return pltpu.with_memory_space_constraint(value, pltpu.HBM)


def attend_call(order, lengths, table, adapters, queries, fresh, down, residual, pool):
    steps, rows, features = queries.shape
    blocks, block_size, width = pool.shape
    table_blocks = table.shape[0]
    positions = table_blocks * block_size
    score_rows = rows * steps * features // (width // 2)
    smem = pl.BlockSpec(memory_space=pltpu.SMEM)
    vmem = pl.BlockSpec(memory_space=pltpu.VMEM)
    hbm = pl.BlockSpec(memory_space=pl.ANY)
    return pl.pallas_call(
        attend_kernel,
        out_shape=(
            pltpu.VMEM((steps * rows // 2, 2 * features + LANES), bf16),
            pltpu.VMEM((steps * rows // 2, 2 * features + LANES), bf16),
            pltpu.VMEM(pool.shape, bf16),
        ),
        in_specs=[smem] * 4 + [hbm] * 5,
        out_specs=(vmem,) * 3,
        scratch_shapes=[
            pltpu.VMEM(queries.shape, bf16),
            pltpu.VMEM(fresh.shape, bf16),
            pltpu.VMEM(down.shape, bf16),
            pltpu.VMEM(residual.shape, bf16),
            pltpu.VMEM((score_rows, positions), f32),
            pltpu.VMEM((score_rows, positions), f32),
            pltpu.VMEM((score_rows, width // 2), f32),
            pltpu.SMEM((rows,), jnp.int32),
            pltpu.SMEM((rows,), jnp.int32),
            pltpu.SemaphoreType.DMA((4,)),
            pltpu.SemaphoreType.DMA,
        ],
        compiler_params=pltpu.CompilerParams(vmem_limit_bytes=2 * SMALL_BYTES),
        cost_estimate=pl.CostEstimate(
            flops=ATTEND_FLOPS, bytes_accessed=4 * pool.size, transcendentals=0
        ),
        name="attend",
    )(*(in_hbm(x) for x in (order, lengths, table, adapters, queries, fresh, down, residual, pool)))


def prepare_call(order, lengths, table, adapters, pool, steps, rows, slots):
    smem = pl.BlockSpec(memory_space=pltpu.SMEM)
    vmem = pl.BlockSpec(memory_space=pltpu.VMEM)
    return pl.pallas_call(
        prepare_kernel,
        out_shape=(
            pltpu.VMEM((rows // 2, table.shape[0]) + pool.shape[1:], bf16),
            pltpu.VMEM((steps * rows, steps * rows), bf16),
            pltpu.VMEM((steps * rows, slots), f32),
        ),
        in_specs=[smem] * 4 + [vmem],
        out_specs=(vmem,) * 3,
        compiler_params=pltpu.CompilerParams(vmem_limit_bytes=SMALL_BYTES),
        cost_estimate=pl.CostEstimate(flops=PREPARE_FLOPS, bytes_accessed=0, transcendentals=0),
        name="prepare",
    )(order, lengths, table, adapters, pool)


def message_call(stay, arrived, weight, partners, dtype):
    tensor = lax.axis_size("tensor")
    spans = tensor // QUAD
    columns = spans * weight.shape[1] // tensor
    vmem = pl.BlockSpec(memory_space=pltpu.VMEM)
    return pl.pallas_call(
        functools.partial(message_kernel, partners=partners),
        out_shape=pltpu.VMEM((2 * stay.shape[0], columns + LANES), dtype),
        in_specs=[vmem] * 3,
        out_specs=vmem,
        compiler_params=pltpu.CompilerParams(vmem_limit_bytes=SMALL_BYTES),
        name="message",
    )(stay, arrived, weight)


def place_call(order, lengths, table, pool, arrived, rows):
    smem = pl.BlockSpec(memory_space=pltpu.SMEM)
    vmem = pl.BlockSpec(memory_space=pltpu.VMEM)
    return pl.pallas_call(
        place_kernel,
        out_shape=jax.ShapeDtypeStruct((rows, table.shape[0]) + pool.shape[1:], bf16),
        in_specs=[smem] * 3 + [vmem] * 2,
        out_specs=pl.BlockSpec(memory_space=pl.ANY),
        scratch_shapes=[pltpu.VMEM(pool.shape[1:], bf16), pltpu.SemaphoreType.DMA],
        compiler_params=pltpu.CompilerParams(vmem_limit_bytes=SMALL_BYTES),
        cost_estimate=pl.CostEstimate(flops=0, bytes_accessed=2 * pool.size, transcendentals=0),
        name="place",
    )(order, lengths, table, pool, arrived)


def merge_kernel(*refs, spans):
    messages, outs = refs[:-spans], refs[-spans:]
    total = messages[0][...]
    for ref in messages[1:]:
        total = total + ref[...].astype(f32)
    out_width = (total.shape[1] - LANES) // spans
    for n, ref in enumerate(outs):
        ref[:, :out_width] = total[:, n * out_width : (n + 1) * out_width].astype(ref.dtype)
        ref[:, out_width:] = total[:, spans * out_width :].astype(ref.dtype)


def merge_call(messages, spans):
    rows, columns = messages[0].shape
    vmem = pl.BlockSpec(memory_space=pltpu.VMEM)
    width = (columns - LANES) // spans + LANES
    return pl.pallas_call(
        functools.partial(merge_kernel, spans=spans),
        out_shape=[pltpu.VMEM((rows, width), f32 if n == 0 else bf16) for n in range(spans)],
        in_specs=[vmem] * len(messages),
        out_specs=[vmem] * spans,
        compiler_params=pltpu.CompilerParams(vmem_limit_bytes=SMALL_BYTES),
        cost_estimate=pl.CostEstimate(flops=MERGE_FLOPS, bytes_accessed=0, transcendentals=0),
        name="merge",
    )(*messages)


def finish_kernel(
    turn_ref, slot_ref, up_ref, other_up_ref, stay_ref, arrived_ref, home_ref, *rest
):
    across_refs, out_ref = rest[:-1], rest[-1]
    slots, rank, features = up_ref.shape
    group = stay_ref.shape[0]
    total = home_ref[...]
    for ref in across_refs:
        total = total + ref[...].astype(f32)
    shrink = total[:, features : features + rank].astype(bf16).astype(f32)
    wide = jnp.concatenate(
        [shrink * slot_ref[:, n : n + 1] for n in range(slots)], axis=1
    ).astype(bf16)
    finished = []
    for side, (up, stream) in enumerate(((up_ref, stay_ref), (other_up_ref, arrived_ref))):
        span = slice(side * group, (side + 1) * group)
        raised = dot(wide[span], up[...].reshape(slots * rank, features))
        residual = stream[:, features + LANES :].astype(f32)
        finished.append(residual + total[span, :features] + adapter_scale * raised)
    finished = jnp.concatenate(finished, axis=0).astype(bf16)
    out_ref[...] = dot(turn_ref[...], finished).astype(bf16).reshape(out_ref.shape)


def shards(
    queries,
    latest_key_value,
    residual,
    paged_cache_pool,
    adapter_down_weight,
    adapter_up_weight,
    output_weight,
    lengths,
    previous_block_table,
    request_order_after,
    request_adapter_index,
):
    steps, rows, features = queries.shape
    replicas = lax.axis_size("replica")
    tensor = lax.axis_size("tensor")
    blocks, _, block_size, width = paged_cache_pool.shape
    table_blocks = previous_block_table.shape[1]
    pool = paged_cache_pool.reshape(blocks, block_size, width)
    fresh = latest_key_value.reshape(steps, rows, width)
    swap = [(0, 1), (1, 0)]
    other_up = lax.ppermute(adapter_up_weight, "replica", swap)

    table = previous_block_table.T
    integers = (request_order_after, lengths, table, request_adapter_index)
    stay, leave, pool = attend_call(
        *integers, queries, fresh, adapter_down_weight, residual, pool
    )
    came = lax.ppermute(leave, "replica", swap)
    leaving, turn, slot = prepare_call(*integers, pool, steps, rows, adapter_up_weight.shape[0])
    spans = tensor // QUAD

    def trade(message, partners):
        pairs = [
            (r * tensor + t, r * tensor + (t ^ partners[r]))
            for r in range(replicas)
            for t in range(tensor)
        ]
        return lax.ppermute(message, ("replica", "tensor"), pairs)

    message = functools.partial(message_call, stay, came, output_weight)
    landed = [trade(message(partners, bf16), partners) for partners in PARTNERS]
    own = message((0, 0), f32)
    arrived = lax.ppermute(leaving, "replica", swap)
    home, *across = merge_call([own] + landed, spans)
    across = [trade(piece, (n * QUAD, n * QUAD)) for n, piece in enumerate(across, 1)]
    placed_cache = place_call(*integers[:3], pool, arrived, rows)
    placed_cache, turn = lax.optimization_barrier((placed_cache, turn))
    vmem = pl.BlockSpec(memory_space=pltpu.VMEM)
    layer_out = pl.pallas_call(
        finish_kernel,
        out_shape=jax.ShapeDtypeStruct((steps, rows, features), bf16),
        in_specs=[vmem] * (7 + len(across)),
        out_specs=vmem,
        compiler_params=pltpu.CompilerParams(vmem_limit_bytes=SMALL_BYTES),
        name="finish",
    )(turn, slot, adapter_up_weight, other_up, stay, came, home, *across)
    return (layer_out, placed_cache.reshape(rows, table_blocks, 1, block_size, width))


def solution(mesh):
    in_specs = (
        P(None, ("groups", "replica"), "tensor"),
        P(None, ("groups", "replica"), "tensor", None),
        P(None, ("groups", "replica"), "tensor"),
        P(("groups", "replica"), "tensor", None, None),
        P(("groups", "replica"), None, "tensor"),
        P(("groups", "replica"), None, "tensor"),
        P("tensor", None),
        P("groups"),
        P("groups", None),
        P("groups"),
        P("groups"),
    )
    out_specs = (
        P(None, ("groups", "replica"), "tensor"),
        P(("groups", "replica"), None, "tensor", None, None),
    )
    return jax.shard_map(shards, mesh=mesh, in_specs=in_specs, out_specs=out_specs, check_vma=False)
```

```python
import functools

import jax
import jax.numpy as jnp
from jax import lax
from jax.experimental import pallas as pl
from jax.experimental.pallas import tpu as pltpu
from jax.sharding import PartitionSpec as P

adapter_scale = 2.0
bf16 = jnp.bfloat16
f32 = jnp.float32
LANES = 128
QUAD = 4
PARTNERS = ((3, 3), (2, 2), (1, 1))
LATE = 0
HOME = (0,)
ATTEND_FLOPS = 40_000_000_000
MERGE_FLOPS = 50_000_000_000
VMEM_BYTES = 56 * 1024 * 1024
SMALL_BYTES = 8 * 1024 * 1024


def iota(shape, dim):
    return lax.broadcasted_iota(jnp.int32, shape, dim)


def div(value, size):
    return value >> (size.bit_length() - 1) if size & (size - 1) == 0 else value // size


def mod(value, size):
    return value & (size - 1) if size & (size - 1) == 0 else value % size


def dot(a, b, contract=((1,), (0,))):
    return lax.dot_general(a, b, (contract, ((), ())), preferred_element_type=f32)


def one_hot(mask):
    return jnp.where(mask, 1.0, 0.0).astype(bf16)


def rank_rows(order_ref, found_ref, target_ref, holder, place, row_count, base):
    def step(j, count):
        request = order_ref[place * row_count + j]
        hit = div(request, row_count) == holder

        @pl.when(hit)
        def _():
            found_ref[base + count] = request - holder * row_count
            target_ref[base + count] = j

        return count + hit.astype(jnp.int32)

    lax.fori_loop(0, row_count, step, jnp.int32(0))


def attend_kernel(
    order_ref,
    lengths_ref,
    table_ref,
    adapter_ref,
    queries_hbm,
    fresh_hbm,
    down_hbm,
    residual_hbm,
    pool_ref,
    stay_ref,
    leave_ref,
    turn_ref,
    slot_ref,
    pool_v,
    queries_ref,
    fresh_ref,
    down_ref,
    residual_ref,
    scores_v,
    probs_v,
    attended_v,
    found,
    target,
    small_sem,
    pool_sem,
):
    steps, rows, features = queries_ref.shape
    blocks, block_size, width = pool_v.shape
    head = width // 2
    heads = features // head
    sh = steps * heads
    table_blocks = table_ref.shape[0]
    positions = table_blocks * block_size
    places = lengths_ref.shape[0] // rows
    half = rows // places
    slots, rank = down_ref.shape[:2]
    me = lax.axis_index("replica")
    first = me * rows

    small_copies = [
        pltpu.make_async_copy(source, target, small_sem.at[n])
        for n, (source, target) in enumerate(
            (
                (queries_hbm, queries_ref),
                (fresh_hbm, fresh_ref),
                (down_hbm, down_ref),
                (residual_hbm, residual_ref),
            )
        )
    ]
    pool_copy = pltpu.make_async_copy(pool_ref, pool_v, pool_sem)
    small_copies[0].start()
    small_copies[1].start()
    pool_copy.start()
    small_copies[2].start()
    small_copies[3].start()

    for place in range(places):
        rank_rows(order_ref, found, target, me, me if place == 0 else 1 - me, rows, place * half)

    small_copies[0].wait()
    small_copies[1].wait()
    stacked = jnp.concatenate(
        [
            queries_ref[s, :, h * head : (h + 1) * head]
            for s in range(steps)
            for h in range(heads)
        ],
        axis=0,
    )
    total = rows * sh
    out_row, in_row = iota((total, total), 0), iota((total, total), 1)
    turn = one_hot((div(out_row, sh) == mod(in_row, rows)) & (mod(out_row, sh) == div(in_row, rows)))
    turned = dot(turn, stacked)
    query_rows = turned.astype(bf16)
    spread = one_hot(div(iota((total, rows), 0), sh) == iota((total, rows), 1))
    scale = head ** (-0.5)
    fresh_rows = [dot(spread, fresh_ref[s]) for s in range(steps)]
    step_of = div(mod(iota((total, 1), 0), sh), heads)
    fresh_scores = []
    for s in range(steps):
        value = jnp.sum(turned * fresh_rows[s][:, :head], axis=1, keepdims=True) * scale
        fresh_scores.append(jnp.where(step_of >= s, value, f32(-1e30)))

    group = steps * half
    row = iota((2 * group, 1), 0)
    step_of, place_of = div(row, rows), mod(row, rows)
    side_of, rank_of = div(row, group), mod(row, half)
    wanted = jnp.zeros_like(row)
    new_adapter = jnp.zeros_like(row)
    counts = [jnp.int32(0), jnp.int32(0)]
    for j in range(rows):
        request = order_ref[me * rows + j]
        away = jnp.where(div(request, rows) == me, 0, 1)
        count = jnp.where(away == 0, counts[0], counts[1])
        counts = [counts[0] + 1 - away, counts[1] + away]
        wanted = jnp.where(place_of == j, away * group + count, wanted)
        here = (side_of == away) & (rank_of == count)
        new_adapter = jnp.where(here, adapter_ref[request], new_adapter)
    wanted = wanted + step_of * half
    turn_ref[...] = one_hot(iota(turn_ref.shape, 1) == wanted)
    slot_ref[...] = one_hot(iota(slot_ref.shape, 1) == new_adapter).astype(f32)

    pool_copy.wait()

    def block_rows(row, lo):
        return jnp.concatenate(
            [pool_v[table_ref[b, first + row], :, lo : lo + head] for b in range(table_blocks)],
            axis=0,
        )

    position = iota((block_size, width), 0)
    for row in range(rows):
        length = lengths_ref[first + row]
        full = div(length, block_size)

        @pl.when(full < table_blocks)
        def _(row=row, length=length, full=full):
            block = table_ref[full, first + row]
            kept = jnp.where(
                position < length - full * block_size, pool_v[block].astype(f32), 0.0
            )
            pool_v[block] = kept.astype(bf16)

    column = iota((sh, positions), 1)
    for row in range(rows):
        part = dot(query_rows[row * sh : (row + 1) * sh], block_rows(row, 0), ((1,), (1,)))
        part = jnp.where(column < lengths_ref[first + row], part * scale, f32(-1e30))
        scores_v[row * sh : (row + 1) * sh, :] = part

    scores = scores_v[...]
    top = jnp.max(scores, axis=1, keepdims=True)
    for value in fresh_scores:
        top = jnp.maximum(top, value)
    weights = jnp.exp(scores - top)
    fresh_weights = [jnp.exp(value - top) for value in fresh_scores]
    totals = jnp.sum(weights, axis=1, keepdims=True)
    for value in fresh_weights:
        totals = totals + value
    probs_v[...] = weights / totals

    for row in range(rows):
        span = slice(row * sh, (row + 1) * sh)
        attended_v[span, :] = dot(probs_v[span, :].astype(bf16), block_rows(row, head))
    attended = attended_v[...]
    for value, row in zip(fresh_weights, fresh_rows):
        share = (value / totals).astype(bf16).astype(f32)
        attended = attended + share * row[:, head:]
    attended = attended.astype(bf16)

    row_index = iota((places * steps * half, 1), 0)
    source = jnp.zeros_like(row_index)
    adapter = jnp.zeros_like(row_index)
    for place in range(places):
        for slot in range(half):
            local = found[place * half + slot]
            here = (div(row_index, steps * half) == place) & (mod(row_index, half) == slot)
            source = jnp.where(here, local, source)
            adapter = jnp.where(here, adapter_ref[first + local], adapter)
    step_index = div(mod(row_index, steps * half), half)
    columns = iota((places * steps * half, total), 1)
    pieces = []
    for h in range(heads):
        wanted = source * sh + step_index * heads + h
        pieces.append(dot(one_hot(columns == wanted), attended))
    mixed = jnp.concatenate(pieces, axis=1).astype(bf16)

    small_copies[2].wait()
    wide = dot(mixed, down_ref[...].reshape(slots * rank, features), ((1,), (1,)))
    shrink = jnp.zeros((places * steps * half, rank), f32)
    for slot in range(slots):
        shrink = shrink + jnp.where(
            adapter == slot, wide[:, slot * rank : (slot + 1) * rank], 0.0
        )
    shrink = jnp.concatenate(
        [shrink, jnp.zeros((places * steps * half, LANES - rank), f32)], axis=1
    ).astype(bf16)

    small_copies[3].wait()
    wanted = step_index * rows + source
    stream = dot(
        one_hot(iota((steps * rows, steps * rows), 1) == wanted),
        residual_ref[...].reshape(steps * rows, features),
    ).astype(bf16)
    group = steps * half
    for place, ref in enumerate((stay_ref, leave_ref)):
        span = slice(place * group, (place + 1) * group)
        ref[:, :features] = mixed[span]
        ref[:, features : features + LANES] = shrink[span]
        ref[:, features + LANES :] = stream[span]


def message_kernel(stay_ref, arrived_ref, weight_ref, message_ref, *, partners, spans):
    out_width = weight_ref.shape[1] // lax.axis_size("tensor")
    features = weight_ref.shape[0]
    here = lax.axis_index("tensor")
    partner = jnp.where(lax.axis_index("replica") == 0, partners[0], partners[1])
    mixed = jnp.concatenate([stay_ref[:, :features], arrived_ref[:, :features]], axis=0)
    for n, span in enumerate(spans):
        start = pl.multiple_of((here ^ (span * QUAD + partner)) * out_width, out_width)
        part = dot(mixed, weight_ref[:, pl.ds(start, out_width)])
        message_ref[:, n * out_width : (n + 1) * out_width] = part.astype(message_ref.dtype)
    if message_ref.shape[1] > len(spans) * out_width:
        group = stay_ref.shape[0]
        for side, ref in enumerate((stay_ref, arrived_ref)):
            shrink = ref[:, features : features + LANES].astype(message_ref.dtype)
            message_ref[side * group : (side + 1) * group, len(spans) * out_width :] = shrink


def place_kernel(order_ref, lengths_ref, table_ref, pool_v, *refs, stayed):
    placed_ref, zero_v, sem = refs[-3:]
    rows, table_blocks, block_size, _ = placed_ref.shape
    me = lax.axis_index("replica")
    zero_v[...] = jnp.zeros_like(zero_v)

    def step(j, carry):
        request = order_ref[me * rows + j]
        length = lengths_ref[request]

        @pl.when((div(request, rows) == me) == stayed)
        def _():
            for b in range(table_blocks):
                target = placed_ref.at[j, b]

                @pl.when(b * block_size < length)
                def _():
                    source = pool_v.at[table_ref[b, request]]
                    pltpu.make_async_copy(source, target, sem).start()

                @pl.when(b * block_size >= length)
                def _():
                    pltpu.make_async_copy(zero_v, target, sem).start()

        return carry

    lax.fori_loop(0, rows, step, 0)
    part = placed_ref.at[pl.ds(0, rows // 2)]
    pltpu.make_async_copy(part, part, sem).wait()


def in_hbm(value):
    return pltpu.with_memory_space_constraint(value, pltpu.HBM)


def attend_call(order, lengths, table, adapters, queries, fresh, down, residual, pool):
    steps, rows, features = queries.shape
    blocks, block_size, width = pool.shape
    table_blocks = table.shape[0]
    positions = table_blocks * block_size
    score_rows = rows * steps * features // (width // 2)
    smem = pl.BlockSpec(memory_space=pltpu.SMEM)
    vmem = pl.BlockSpec(memory_space=pltpu.VMEM)
    hbm = pl.BlockSpec(memory_space=pl.ANY)
    return pl.pallas_call(
        attend_kernel,
        out_shape=(
            pltpu.VMEM((steps * rows // 2, 2 * features + LANES), bf16),
            pltpu.VMEM((steps * rows // 2, 2 * features + LANES), bf16),
            pltpu.VMEM((steps * rows, steps * rows), bf16),
            pltpu.VMEM((steps * rows, down.shape[0]), f32),
            pltpu.VMEM(pool.shape, bf16),
        ),
        in_specs=[smem] * 4 + [hbm] * 5,
        out_specs=(vmem,) * 5,
        scratch_shapes=[
            pltpu.VMEM(queries.shape, bf16),
            pltpu.VMEM(fresh.shape, bf16),
            pltpu.VMEM(down.shape, bf16),
            pltpu.VMEM(residual.shape, bf16),
            pltpu.VMEM((score_rows, positions), f32),
            pltpu.VMEM((score_rows, positions), f32),
            pltpu.VMEM((score_rows, width // 2), f32),
            pltpu.SMEM((rows,), jnp.int32),
            pltpu.SMEM((rows,), jnp.int32),
            pltpu.SemaphoreType.DMA((4,)),
            pltpu.SemaphoreType.DMA,
        ],
        compiler_params=pltpu.CompilerParams(vmem_limit_bytes=2 * SMALL_BYTES),
        cost_estimate=pl.CostEstimate(
            flops=ATTEND_FLOPS, bytes_accessed=4 * pool.size, transcendentals=0
        ),
        name="attend",
    )(*(in_hbm(x) for x in (order, lengths, table, adapters, queries, fresh, down, residual, pool)))


def message_call(stay, arrived, weight, partners, spans, dtype):
    out_width = weight.shape[1] // lax.axis_size("tensor")
    columns = len(spans) * out_width + (0 if spans == HOME else LANES)
    vmem = pl.BlockSpec(memory_space=pltpu.VMEM)
    return pl.pallas_call(
        functools.partial(message_kernel, partners=partners, spans=spans),
        out_shape=pltpu.VMEM((2 * stay.shape[0], columns), dtype),
        in_specs=[vmem] * 3,
        out_specs=vmem,
        compiler_params=pltpu.CompilerParams(vmem_limit_bytes=SMALL_BYTES),
        name="message",
    )(stay, arrived, weight)


def place_call(order, lengths, table, pool, rows, placed=None):
    smem = pl.BlockSpec(memory_space=pltpu.SMEM)
    vmem = pl.BlockSpec(memory_space=pltpu.VMEM)
    hbm = pl.BlockSpec(memory_space=pl.ANY)
    before = [] if placed is None else [placed]
    return pl.pallas_call(
        functools.partial(place_kernel, stayed=placed is None),
        out_shape=jax.ShapeDtypeStruct((rows, table.shape[0]) + pool.shape[1:], bf16),
        in_specs=[smem] * 3 + [vmem] + [hbm] * len(before),
        out_specs=hbm,
        scratch_shapes=[pltpu.VMEM(pool.shape[1:], bf16), pltpu.SemaphoreType.DMA],
        input_output_aliases={4: 0} if before else {},
        compiler_params=pltpu.CompilerParams(vmem_limit_bytes=SMALL_BYTES),
        cost_estimate=pl.CostEstimate(flops=0, bytes_accessed=2 * pool.size, transcendentals=0),
        name="place",
    )(order, lengths, table, pool, *before)


def merge_kernel(*refs, spans, out_width):
    messages, outs, shrink_ref = refs[:-spans], refs[-spans:-1], refs[-1]
    columns = (spans - 1) * out_width + LANES
    total = messages[0][:, out_width:]
    for ref in messages[1:]:
        total = total + ref[:, ref.shape[1] - columns :].astype(f32)
    shrink = total[:, (spans - 1) * out_width :]
    shrink_ref[...] = shrink
    for n, ref in enumerate(outs):
        ref[:, :out_width] = total[:, n * out_width : (n + 1) * out_width].astype(bf16)
        ref[:, out_width:] = shrink.astype(bf16)


def merge_call(messages, spans):
    rows, columns = messages[0].shape
    vmem = pl.BlockSpec(memory_space=pltpu.VMEM)
    out_width = (columns - LANES) // spans
    return pl.pallas_call(
        functools.partial(merge_kernel, spans=spans, out_width=out_width),
        out_shape=[pltpu.VMEM((rows, out_width + LANES), bf16)] * (spans - 1)
        + [pltpu.VMEM((rows, LANES), f32)],
        in_specs=[vmem] * len(messages),
        out_specs=[vmem] * spans,
        compiler_params=pltpu.CompilerParams(vmem_limit_bytes=SMALL_BYTES),
        cost_estimate=pl.CostEstimate(flops=MERGE_FLOPS, bytes_accessed=0, transcendentals=0),
        name="merge",
    )(*messages)


def finish_kernel(
    turn_ref, slot_ref, up_ref, other_up_ref, stay_ref, arrived_ref, shrink_ref, *rest, home_count
):
    home_refs, across_refs, out_ref = rest[:home_count], rest[home_count:-1], rest[-1]
    slots, rank, features = up_ref.shape
    group = stay_ref.shape[0]
    total, shrink = home_refs[0][:, :features], shrink_ref[:, :rank]
    for ref in home_refs[1:]:
        total = total + ref[:, :features].astype(f32)
    for ref in across_refs:
        total = total + ref[:, :features].astype(f32)
        shrink = shrink + ref[:, features : features + rank].astype(f32)
    shrink = shrink.astype(bf16).astype(f32)
    wide = jnp.concatenate(
        [shrink * slot_ref[:, n : n + 1] for n in range(slots)], axis=1
    ).astype(bf16)
    finished = []
    for side, (up, stream) in enumerate(((up_ref, stay_ref), (other_up_ref, arrived_ref))):
        span = slice(side * group, (side + 1) * group)
        raised = dot(wide[span], up[...].reshape(slots * rank, features))
        residual = stream[:, features + LANES :].astype(f32)
        finished.append(residual + total[span] + adapter_scale * raised)
    finished = jnp.concatenate(finished, axis=0).astype(bf16)
    out_ref[...] = dot(turn_ref[...], finished).astype(bf16).reshape(out_ref.shape)


def shards(
    queries,
    latest_key_value,
    residual,
    paged_cache_pool,
    adapter_down_weight,
    adapter_up_weight,
    output_weight,
    lengths,
    previous_block_table,
    request_order_after,
    request_adapter_index,
):
    steps, rows, features = queries.shape
    replicas = lax.axis_size("replica")
    tensor = lax.axis_size("tensor")
    blocks, _, block_size, width = paged_cache_pool.shape
    table_blocks = previous_block_table.shape[1]
    pool = paged_cache_pool.reshape(blocks, block_size, width)
    fresh = latest_key_value.reshape(steps, rows, width)
    swap = [(0, 1), (1, 0)]
    other_up = lax.ppermute(adapter_up_weight, "replica", swap)

    table = previous_block_table.T
    integers = (request_order_after, lengths, table, request_adapter_index)
    stay, leave, turn, slot, pool = attend_call(
        *integers, queries, fresh, adapter_down_weight, residual, pool
    )
    came = lax.ppermute(leave, "replica", swap)
    spans = tensor // QUAD
    def trade(message, partners):
        pairs = [
            (r * tensor + t, r * tensor + (t ^ partners[r]))
            for r in range(replicas)
            for t in range(tensor)
        ]
        return lax.ppermute(message, ("replica", "tensor"), pairs)

    def message(came, partners, chosen, dtype=bf16):
        return message_call(stay, came, output_weight, partners, chosen, dtype)

    every = tuple(range(spans))
    early = len(PARTNERS) - LATE
    sent = [
        message(came, partners, every if n < early else every[1:])
        for n, partners in enumerate(PARTNERS)
    ]
    collected = [trade(*item) for item in zip(sent, PARTNERS)]
    own = message(came, (0, 0), every, f32)
    came_later, *_ = lax.optimization_barrier((came, *sent))
    home = [own] + collected[:early]
    home += [trade(message(came_later, partners, HOME), partners) for partners in PARTNERS[early:]]
    other_pool = lax.ppermute(pool, "replica", swap)
    placed = place_call(*integers[:3], pool, rows)
    placed, own = lax.optimization_barrier((placed, own))
    home[0] = own
    *across, shrink = merge_call([own] + collected, spans)
    across = [trade(piece, (n * QUAD, n * QUAD)) for n, piece in enumerate(across, 1)]
    placed_cache = place_call(*integers[:3], other_pool, rows, placed)
    placed_cache, turn = lax.optimization_barrier((placed_cache, turn))
    vmem = pl.BlockSpec(memory_space=pltpu.VMEM)
    layer_out = pl.pallas_call(
        functools.partial(finish_kernel, home_count=len(home)),
        out_shape=jax.ShapeDtypeStruct((steps, rows, features), bf16),
        in_specs=[vmem] * (7 + len(home) + len(across)),
        out_specs=vmem,
        compiler_params=pltpu.CompilerParams(vmem_limit_bytes=SMALL_BYTES),
        name="finish",
    )(turn, slot, adapter_up_weight, other_up, stay, came, shrink, *home, *across)
    return (layer_out, placed_cache.reshape(rows, table_blocks, 1, block_size, width))


def solution(mesh):
    in_specs = (
        P(None, ("groups", "replica"), "tensor"),
        P(None, ("groups", "replica"), "tensor", None),
        P(None, ("groups", "replica"), "tensor"),
        P(("groups", "replica"), "tensor", None, None),
        P(("groups", "replica"), None, "tensor"),
        P(("groups", "replica"), None, "tensor"),
        P("tensor", None),
        P("groups"),
        P("groups", None),
        P("groups"),
        P("groups"),
    )
    out_specs = (
        P(None, ("groups", "replica"), "tensor"),
        P(("groups", "replica"), None, "tensor", None, None),
    )
    return jax.shard_map(shards, mesh=mesh, in_specs=in_specs, out_specs=out_specs, check_vma=False)
```

```python
import functools

import jax
import jax.numpy as jnp
from jax import lax
from jax.experimental import pallas as pl
from jax.experimental.pallas import tpu as pltpu
from jax.sharding import PartitionSpec as P

adapter_scale = 2.0
bf16 = jnp.bfloat16
f32 = jnp.float32
LANES = 128
QUAD = 4
PARTNERS = ((3, 3), (2, 2), (1, 1))
ATTEND_FLOPS = 40_000_000_000
MERGE_FLOPS = 50_000_000_000
VMEM_BYTES = 56 * 1024 * 1024
SMALL_BYTES = 8 * 1024 * 1024


def iota(shape, dim):
    return lax.broadcasted_iota(jnp.int32, shape, dim)


def div(value, size):
    return value >> (size.bit_length() - 1) if size & (size - 1) == 0 else value // size


def mod(value, size):
    return value & (size - 1) if size & (size - 1) == 0 else value % size


def dot(a, b, contract=((1,), (0,))):
    return lax.dot_general(a, b, (contract, ((), ())), preferred_element_type=f32)


def one_hot(mask):
    return jnp.where(mask, 1.0, 0.0).astype(bf16)


def rank_rows(order_ref, found_ref, target_ref, holder, place, row_count, base):
    def step(j, count):
        request = order_ref[place * row_count + j]
        hit = div(request, row_count) == holder

        @pl.when(hit)
        def _():
            found_ref[base + count] = request - holder * row_count
            target_ref[base + count] = j

        return count + hit.astype(jnp.int32)

    lax.fori_loop(0, row_count, step, jnp.int32(0))


def attend_kernel(
    order_ref,
    lengths_ref,
    table_ref,
    adapter_ref,
    queries_hbm,
    fresh_hbm,
    down_hbm,
    residual_hbm,
    pool_ref,
    stay_ref,
    leave_ref,
    turn_ref,
    slot_ref,
    pool_v,
    queries_ref,
    fresh_ref,
    down_ref,
    residual_ref,
    scores_v,
    probs_v,
    attended_v,
    back_v,
    found,
    target,
    small_sem,
    pool_sem,
):
    steps, rows, features = queries_ref.shape
    blocks, block_size, width = pool_v.shape
    head = width // 2
    heads = features // head
    sh = steps * heads
    table_blocks = table_ref.shape[0]
    positions = table_blocks * block_size
    places = lengths_ref.shape[0] // rows
    half = rows // places
    slots, rank = down_ref.shape[:2]
    me = lax.axis_index("replica")
    first = me * rows

    small_copies = [
        pltpu.make_async_copy(source, target, small_sem.at[n])
        for n, (source, target) in enumerate(
            (
                (queries_hbm, queries_ref),
                (fresh_hbm, fresh_ref),
                (down_hbm, down_ref),
                (residual_hbm, residual_ref),
            )
        )
    ]
    pool_copy = pltpu.make_async_copy(pool_ref, pool_v, pool_sem)
    pool_copy.start()
    for copy in small_copies:
        copy.start()

    for place in range(places):
        rank_rows(order_ref, found, target, me, me if place == 0 else 1 - me, rows, place * half)

    small_copies[0].wait()
    small_copies[1].wait()
    stacked = jnp.concatenate(
        [
            queries_ref[s, :, h * head : (h + 1) * head]
            for s in range(steps)
            for h in range(heads)
        ],
        axis=0,
    )
    total = rows * sh
    out_row, in_row = iota((total, total), 0), iota((total, total), 1)
    turn = one_hot((div(out_row, sh) == mod(in_row, rows)) & (mod(out_row, sh) == div(in_row, rows)))
    turned = dot(turn, stacked)
    query_rows = turned.astype(bf16)
    spread = one_hot(div(iota((total, rows), 0), sh) == iota((total, rows), 1))
    scale = head ** (-0.5)
    fresh_rows = [dot(spread, fresh_ref[s]) for s in range(steps)]
    step_of = div(mod(iota((total, 1), 0), sh), heads)
    fresh_scores = []
    for s in range(steps):
        value = jnp.sum(turned * fresh_rows[s][:, :head], axis=1, keepdims=True) * scale
        fresh_scores.append(jnp.where(step_of >= s, value, f32(-1e30)))

    group = steps * half
    row = iota((2 * group, 1), 0)
    step_of, place_of = div(row, rows), mod(row, rows)
    wanted = jnp.zeros_like(row)
    slot_of = jnp.zeros_like(row)
    counts = [jnp.int32(0), jnp.int32(0)]
    for j in range(rows):
        request = order_ref[me * rows + j]
        away = jnp.where(div(request, rows) == me, 0, 1)
        count = jnp.where(away == 0, counts[0], counts[1])
        counts = [counts[0] + 1 - away, counts[1] + away]
        here = place_of == j
        wanted = jnp.where(here, away * group + count, wanted)
        slot_of = jnp.where(here, away * slots + adapter_ref[request], slot_of)
    wanted = wanted + step_of * half
    turn_ref[...] = one_hot(iota(turn_ref.shape, 1) == wanted)
    slot_ref[...] = one_hot(iota(slot_ref.shape, 1) == slot_of).astype(f32)

    row_index = iota((places * steps * half, 1), 0)
    source = jnp.zeros_like(row_index)
    adapter = jnp.zeros_like(row_index)
    for place in range(places):
        for slot in range(half):
            local = found[place * half + slot]
            here = (div(row_index, steps * half) == place) & (mod(row_index, half) == slot)
            source = jnp.where(here, local, source)
            adapter = jnp.where(here, adapter_ref[first + local], adapter)
    step_index = div(mod(row_index, steps * half), half)
    columns = iota((places * steps * half, total), 1)
    for h in range(heads):
        wanted = source * sh + step_index * heads + h
        span = slice(h * places * steps * half, (h + 1) * places * steps * half)
        back_v[span, :] = one_hot(columns == wanted)

    small_copies[3].wait()
    wanted = step_index * rows + source
    stream = dot(
        one_hot(iota((steps * rows, steps * rows), 1) == wanted),
        residual_ref[...].reshape(steps * rows, features),
    ).astype(bf16)
    for place, ref in enumerate((stay_ref, leave_ref)):
        span = slice(place * steps * half, (place + 1) * steps * half)
        ref[:, features + LANES :] = stream[span]

    pool_copy.wait()

    def block_rows(row, lo):
        return jnp.concatenate(
            [pool_v[table_ref[b, first + row], :, lo : lo + head] for b in range(table_blocks)],
            axis=0,
        )

    column = iota((sh, positions), 1)
    for row in range(rows):
        part = dot(query_rows[row * sh : (row + 1) * sh], block_rows(row, 0), ((1,), (1,)))
        part = jnp.where(column < lengths_ref[first + row], part * scale, f32(-1e30))
        scores_v[row * sh : (row + 1) * sh, :] = part

    scores = scores_v[...]
    top = jnp.max(scores, axis=1, keepdims=True)
    for value in fresh_scores:
        top = jnp.maximum(top, value)
    weights = jnp.exp(scores - top)
    fresh_weights = [jnp.exp(value - top) for value in fresh_scores]
    totals = jnp.sum(weights, axis=1, keepdims=True)
    for value in fresh_weights:
        totals = totals + value
    probs_v[...] = weights / totals

    for row in range(rows):
        span = slice(row * sh, (row + 1) * sh)
        attended_v[span, :] = dot(probs_v[span, :].astype(bf16), block_rows(row, head))
    attended = attended_v[...]
    for value, row in zip(fresh_weights, fresh_rows):
        share = (value / totals).astype(bf16).astype(f32)
        attended = attended + share * row[:, head:]
    attended = attended.astype(bf16)

    turned = dot(back_v[...], attended)
    count = places * steps * half
    mixed = jnp.concatenate(
        [turned[h * count : (h + 1) * count] for h in range(heads)], axis=1
    ).astype(bf16)

    small_copies[2].wait()
    wide = dot(mixed, down_ref[...].reshape(slots * rank, features), ((1,), (1,)))
    shrink = jnp.zeros((places * steps * half, rank), f32)
    for slot in range(slots):
        shrink = shrink + jnp.where(
            adapter == slot, wide[:, slot * rank : (slot + 1) * rank], 0.0
        )
    shrink = jnp.concatenate(
        [shrink, jnp.zeros((places * steps * half, LANES - rank), f32)], axis=1
    ).astype(bf16)

    group = steps * half
    for place, ref in enumerate((stay_ref, leave_ref)):
        span = slice(place * group, (place + 1) * group)
        ref[:, :features] = mixed[span]
        ref[:, features : features + LANES] = shrink[span]


def sort_kernel(turn_ref, stay_ref, came_ref, out_ref):
    out_ref[...] = dot(
        turn_ref[...], jnp.concatenate([stay_ref[...], came_ref[...]], axis=0)
    ).astype(bf16)


def sort_call(turn, stay, came):
    vmem = pl.BlockSpec(memory_space=pltpu.VMEM)
    return pl.pallas_call(
        sort_kernel,
        out_shape=pltpu.VMEM((turn.shape[0], stay.shape[1]), bf16),
        in_specs=[vmem] * 3,
        out_specs=vmem,
        compiler_params=pltpu.CompilerParams(vmem_limit_bytes=SMALL_BYTES),
        name="sort",
    )(turn, stay, came)


def message_kernel(rows_ref, came_ref, weight_ref, message_ref, *, partners):
    out_width = weight_ref.shape[1] // lax.axis_size("tensor")
    features = weight_ref.shape[0]
    spans = message_ref.shape[1] // out_width
    here = lax.axis_index("tensor")
    partner = jnp.where(lax.axis_index("replica") == 0, partners[0], partners[1])
    mixed = rows_ref[:, :features]
    for span in range(spans):
        start = pl.multiple_of((here ^ (span * QUAD + partner)) * out_width, out_width)
        part = dot(mixed, weight_ref[:, pl.ds(start, out_width)])
        message_ref[:, span * out_width : (span + 1) * out_width] = part.astype(message_ref.dtype)
    shrink = rows_ref[:, features : features + LANES]
    message_ref[:, spans * out_width :] = shrink.astype(message_ref.dtype)


def place_kernel(order_ref, lengths_ref, table_ref, pool_v, *refs, stayed):
    placed_ref, zero_v, edge_v, sem = refs[-4:]
    rows, table_blocks, block_size, _ = placed_ref.shape
    me = lax.axis_index("replica")
    zero_v[...] = jnp.zeros_like(zero_v)
    position = iota(zero_v.shape, 0)

    def step(j, count):
        request = order_ref[me * rows + j]
        length = lengths_ref[request]
        full = div(length, block_size)
        hit = (div(request, rows) == me) == stayed

        @pl.when(hit)
        def _():
            @pl.when(full < table_blocks)
            def _():
                block = table_ref[jnp.minimum(full, table_blocks - 1), request]
                kept = position < length - full * block_size
                edge_v[count] = jnp.where(kept, pool_v[block].astype(f32), 0.0).astype(bf16)

            for b in range(table_blocks):
                target = placed_ref.at[j, b]

                @pl.when(b < full)
                def _():
                    source = pool_v.at[table_ref[b, request]]
                    pltpu.make_async_copy(source, target, sem).start()

                @pl.when(b == full)
                def _():
                    pltpu.make_async_copy(edge_v.at[count], target, sem).start()

                @pl.when(b > full)
                def _():
                    pltpu.make_async_copy(zero_v, target, sem).start()

        return count + hit.astype(jnp.int32)

    lax.fori_loop(0, rows, step, jnp.int32(0))
    part = placed_ref.at[pl.ds(0, rows // 2)]
    pltpu.make_async_copy(part, part, sem).wait()


def in_hbm(value):
    return pltpu.with_memory_space_constraint(value, pltpu.HBM)


def attend_call(order, lengths, table, adapters, queries, fresh, down, residual, pool):
    steps, rows, features = queries.shape
    blocks, block_size, width = pool.shape
    table_blocks = table.shape[0]
    positions = table_blocks * block_size
    score_rows = rows * steps * features // (width // 2)
    smem = pl.BlockSpec(memory_space=pltpu.SMEM)
    vmem = pl.BlockSpec(memory_space=pltpu.VMEM)
    hbm = pl.BlockSpec(memory_space=pl.ANY)
    return pl.pallas_call(
        attend_kernel,
        out_shape=(
            pltpu.VMEM((steps * rows // 2, 2 * features + LANES), bf16),
            pltpu.VMEM((steps * rows // 2, 2 * features + LANES), bf16),
            pltpu.VMEM((steps * rows, steps * rows), bf16),
            pltpu.VMEM((steps * rows, 2 * down.shape[0]), f32),
            pltpu.VMEM(pool.shape, bf16),
        ),
        in_specs=[smem] * 4 + [hbm] * 5,
        out_specs=(vmem,) * 5,
        scratch_shapes=[
            pltpu.VMEM(queries.shape, bf16),
            pltpu.VMEM(fresh.shape, bf16),
            pltpu.VMEM(down.shape, bf16),
            pltpu.VMEM(residual.shape, bf16),
            pltpu.VMEM((score_rows, positions), f32),
            pltpu.VMEM((score_rows, positions), f32),
            pltpu.VMEM((score_rows, width // 2), f32),
            pltpu.VMEM((features // (width // 2) * steps * rows, score_rows), bf16),
            pltpu.SMEM((rows,), jnp.int32),
            pltpu.SMEM((rows,), jnp.int32),
            pltpu.SemaphoreType.DMA((4,)),
            pltpu.SemaphoreType.DMA,
        ],
        compiler_params=pltpu.CompilerParams(vmem_limit_bytes=2 * SMALL_BYTES),
        cost_estimate=pl.CostEstimate(
            flops=ATTEND_FLOPS, bytes_accessed=4 * pool.size, transcendentals=0
        ),
        name="attend",
    )(*(in_hbm(x) for x in (order, lengths, table, adapters, queries, fresh, down, residual, pool)))


def message_call(rows, came, weight, partners, dtype):
    tensor = lax.axis_size("tensor")
    columns = tensor // QUAD * weight.shape[1] // tensor
    vmem = pl.BlockSpec(memory_space=pltpu.VMEM)
    return pl.pallas_call(
        functools.partial(message_kernel, partners=partners),
        out_shape=pltpu.VMEM((rows.shape[0], columns + LANES), dtype),
        in_specs=[vmem] * 3,
        out_specs=vmem,
        compiler_params=pltpu.CompilerParams(vmem_limit_bytes=SMALL_BYTES),
        name="message",
    )(rows, came, weight)


def place_call(order, lengths, table, pool, rows, placed=None):
    smem = pl.BlockSpec(memory_space=pltpu.SMEM)
    vmem = pl.BlockSpec(memory_space=pltpu.VMEM)
    hbm = pl.BlockSpec(memory_space=pl.ANY)
    before = [] if placed is None else [placed]
    return pl.pallas_call(
        functools.partial(place_kernel, stayed=placed is None),
        out_shape=jax.ShapeDtypeStruct((rows, table.shape[0]) + pool.shape[1:], bf16),
        in_specs=[smem] * 3 + [vmem] + [hbm] * len(before),
        out_specs=hbm,
        scratch_shapes=[
            pltpu.VMEM(pool.shape[1:], bf16),
            pltpu.VMEM((rows // 2,) + pool.shape[1:], bf16),
            pltpu.SemaphoreType.DMA,
        ],
        input_output_aliases={4: 0} if before else {},
        compiler_params=pltpu.CompilerParams(vmem_limit_bytes=SMALL_BYTES),
        cost_estimate=pl.CostEstimate(flops=0, bytes_accessed=2 * pool.size, transcendentals=0),
        name="place",
    )(order, lengths, table, pool, *before)


def merge_kernel(*refs, spans, out_width):
    messages, outs, shrink_ref = refs[:-spans], refs[-spans:-1], refs[-1]
    columns = (spans - 1) * out_width + LANES
    total = messages[0][:, out_width:]
    for ref in messages[1:]:
        total = total + ref[:, ref.shape[1] - columns :].astype(f32)
    shrink = total[:, (spans - 1) * out_width :]
    shrink_ref[...] = shrink
    for n, ref in enumerate(outs):
        ref[:, :out_width] = total[:, n * out_width : (n + 1) * out_width].astype(bf16)
        ref[:, out_width:] = shrink.astype(bf16)


def merge_call(messages, spans):
    rows, columns = messages[0].shape
    vmem = pl.BlockSpec(memory_space=pltpu.VMEM)
    out_width = (columns - LANES) // spans
    return pl.pallas_call(
        functools.partial(merge_kernel, spans=spans, out_width=out_width),
        out_shape=[pltpu.VMEM((rows, out_width + LANES), bf16)] * (spans - 1)
        + [pltpu.VMEM((rows, LANES), f32)],
        in_specs=[vmem] * len(messages),
        out_specs=[vmem] * spans,
        compiler_params=pltpu.CompilerParams(vmem_limit_bytes=SMALL_BYTES),
        cost_estimate=pl.CostEstimate(flops=MERGE_FLOPS, bytes_accessed=0, transcendentals=0),
        name="merge",
    )(*messages)


def finish_kernel(slot_ref, up_ref, other_up_ref, rows_ref, shrink_ref, *rest, home_count):
    home_refs, across_refs, out_ref = rest[:home_count], rest[home_count:-1], rest[-1]
    slots, rank, features = up_ref.shape
    total, shrink = home_refs[0][:, :features], shrink_ref[:, :rank]
    for ref in home_refs[1:]:
        total = total + ref[:, :features].astype(f32)
    for ref in across_refs:
        total = total + ref[:, :features].astype(f32)
        shrink = shrink + ref[:, features : features + rank].astype(f32)
    shrink = shrink.astype(bf16).astype(f32)
    result = total + rows_ref[:, features + LANES :].astype(f32)
    for side, up in enumerate((up_ref, other_up_ref)):
        wide = jnp.concatenate(
            [shrink * slot_ref[:, side * slots + n : side * slots + n + 1] for n in range(slots)],
            axis=1,
        ).astype(bf16)
        result = result + adapter_scale * dot(wide, up[...].reshape(slots * rank, features))
    out_ref[...] = result.astype(bf16).reshape(out_ref.shape)


def shards(
    queries,
    latest_key_value,
    residual,
    paged_cache_pool,
    adapter_down_weight,
    adapter_up_weight,
    output_weight,
    lengths,
    previous_block_table,
    request_order_after,
    request_adapter_index,
):
    steps, rows, features = queries.shape
    replicas = lax.axis_size("replica")
    tensor = lax.axis_size("tensor")
    blocks, _, block_size, width = paged_cache_pool.shape
    table_blocks = previous_block_table.shape[1]
    pool = paged_cache_pool.reshape(blocks, block_size, width)
    fresh = latest_key_value.reshape(steps, rows, width)
    swap = [(0, 1), (1, 0)]
    other_up = lax.ppermute(adapter_up_weight, "replica", swap)

    table = previous_block_table.T
    integers = (request_order_after, lengths, table, request_adapter_index)
    stay, leave, turn, slot, pool = attend_call(
        *integers, queries, fresh, adapter_down_weight, residual, pool
    )
    came = lax.ppermute(leave, "replica", swap)
    rows_in_order = sort_call(turn, stay, came)
    spans = tensor // QUAD
    def trade(message, partners):
        pairs = [
            (r * tensor + t, r * tensor + (t ^ partners[r]))
            for r in range(replicas)
            for t in range(tensor)
        ]
        return lax.ppermute(message, ("replica", "tensor"), pairs)

    collected = [
        trade(message_call(rows_in_order, came, output_weight, partners, bf16), partners)
        for partners in PARTNERS
    ]
    own = message_call(rows_in_order, came, output_weight, (0, 0), f32)
    home = [own] + collected
    other_pool = lax.ppermute(pool, "replica", swap)
    placed = place_call(*integers[:3], pool, rows)
    placed, own = lax.optimization_barrier((placed, own))
    home[0] = own
    *across, shrink = merge_call([own] + collected, spans)
    across = [trade(piece, (n * QUAD, n * QUAD)) for n, piece in enumerate(across, 1)]
    placed_cache = place_call(*integers[:3], other_pool, rows, placed)
    placed_cache, slot = lax.optimization_barrier((placed_cache, slot))
    vmem = pl.BlockSpec(memory_space=pltpu.VMEM)
    layer_out = pl.pallas_call(
        functools.partial(finish_kernel, home_count=len(home)),
        out_shape=jax.ShapeDtypeStruct((steps, rows, features), bf16),
        in_specs=[vmem] * (5 + len(home) + len(across)),
        out_specs=vmem,
        compiler_params=pltpu.CompilerParams(vmem_limit_bytes=SMALL_BYTES),
        name="finish",
    )(slot, adapter_up_weight, other_up, rows_in_order, shrink, *home, *across)
    return (layer_out, placed_cache.reshape(rows, table_blocks, 1, block_size, width))


def solution(mesh):
    in_specs = (
        P(None, ("groups", "replica"), "tensor"),
        P(None, ("groups", "replica"), "tensor", None),
        P(None, ("groups", "replica"), "tensor"),
        P(("groups", "replica"), "tensor", None, None),
        P(("groups", "replica"), None, "tensor"),
        P(("groups", "replica"), None, "tensor"),
        P("tensor", None),
        P("groups"),
        P("groups", None),
        P("groups"),
        P("groups"),
    )
    out_specs = (
        P(None, ("groups", "replica"), "tensor"),
        P(("groups", "replica"), None, "tensor", None, None),
    )
    return jax.shard_map(shards, mesh=mesh, in_specs=in_specs, out_specs=out_specs, check_vma=False)
```

```python
import functools

import jax
import jax.numpy as jnp
from jax import lax
from jax.experimental import pallas as pl
from jax.experimental.pallas import tpu as pltpu
from jax.sharding import PartitionSpec as P

adapter_scale = 2.0
bf16 = jnp.bfloat16
f32 = jnp.float32
LANES = 128
QUAD = 4
PARTNERS = ((3, 3), (2, 2), (1, 1))
ATTEND_FLOPS = 40_000_000_000
MERGE_FLOPS = 50_000_000_000
VMEM_BYTES = 56 * 1024 * 1024
SMALL_BYTES = 8 * 1024 * 1024


def iota(shape, dim):
    return lax.broadcasted_iota(jnp.int32, shape, dim)


def div(value, size):
    return value >> (size.bit_length() - 1) if size & (size - 1) == 0 else value // size


def mod(value, size):
    return value & (size - 1) if size & (size - 1) == 0 else value % size


def dot(a, b, contract=((1,), (0,))):
    return lax.dot_general(a, b, (contract, ((), ())), preferred_element_type=f32)


def one_hot(mask):
    return jnp.where(mask, 1.0, 0.0).astype(bf16)


def rank_rows(order_ref, found_ref, target_ref, holder, place, row_count, base):
    def step(j, count):
        request = order_ref[place * row_count + j]
        hit = div(request, row_count) == holder

        @pl.when(hit)
        def _():
            found_ref[base + count] = request - holder * row_count
            target_ref[base + count] = j

        return count + hit.astype(jnp.int32)

    lax.fori_loop(0, row_count, step, jnp.int32(0))


def attend_kernel(
    order_ref,
    lengths_ref,
    table_ref,
    adapter_ref,
    queries_hbm,
    fresh_hbm,
    down_hbm,
    residual_hbm,
    pool_ref,
    stay_ref,
    leave_ref,
    turn_ref,
    slot_ref,
    pool_v,
    queries_ref,
    fresh_ref,
    down_ref,
    residual_ref,
    scores_v,
    probs_v,
    attended_v,
    back_v,
    found,
    target,
    small_sem,
    pool_sem,
):
    steps, rows, features = queries_ref.shape
    blocks, block_size, width = pool_v.shape
    head = width // 2
    heads = features // head
    sh = steps * heads
    table_blocks = table_ref.shape[0]
    positions = table_blocks * block_size
    places = lengths_ref.shape[0] // rows
    half = rows // places
    slots, rank = down_ref.shape[:2]
    me = lax.axis_index("replica")
    first = me * rows

    small_copies = [
        pltpu.make_async_copy(source, target, small_sem.at[n])
        for n, (source, target) in enumerate(
            (
                (queries_hbm, queries_ref),
                (fresh_hbm, fresh_ref),
                (down_hbm, down_ref),
                (residual_hbm, residual_ref),
            )
        )
    ]
    pool_copy = pltpu.make_async_copy(pool_ref, pool_v, pool_sem)
    pool_copy.start()
    for copy in small_copies:
        copy.start()

    for place in range(places):
        rank_rows(order_ref, found, target, me, me if place == 0 else 1 - me, rows, place * half)

    small_copies[0].wait()
    small_copies[1].wait()
    stacked = jnp.concatenate(
        [
            queries_ref[s, :, h * head : (h + 1) * head]
            for s in range(steps)
            for h in range(heads)
        ],
        axis=0,
    )
    total = rows * sh
    out_row, in_row = iota((total, total), 0), iota((total, total), 1)
    turn = one_hot((div(out_row, sh) == mod(in_row, rows)) & (mod(out_row, sh) == div(in_row, rows)))
    turned = dot(turn, stacked)
    query_rows = turned.astype(bf16)
    spread = one_hot(div(iota((total, rows), 0), sh) == iota((total, rows), 1))
    scale = head ** (-0.5)
    fresh_rows = [dot(spread, fresh_ref[s]) for s in range(steps)]
    step_of = div(mod(iota((total, 1), 0), sh), heads)
    fresh_scores = []
    for s in range(steps):
        value = jnp.sum(turned * fresh_rows[s][:, :head], axis=1, keepdims=True) * scale
        fresh_scores.append(jnp.where(step_of >= s, value, f32(-1e30)))

    group = steps * half
    row = iota((2 * group, 1), 0)
    step_of, place_of = div(row, rows), mod(row, rows)
    wanted = jnp.zeros_like(row)
    slot_of = jnp.zeros_like(row)
    counts = [jnp.int32(0), jnp.int32(0)]
    for j in range(rows):
        request = order_ref[me * rows + j]
        away = jnp.where(div(request, rows) == me, 0, 1)
        count = jnp.where(away == 0, counts[0], counts[1])
        counts = [counts[0] + 1 - away, counts[1] + away]
        here = place_of == j
        wanted = jnp.where(here, away * group + count, wanted)
        slot_of = jnp.where(here, away * slots + adapter_ref[request], slot_of)
    wanted = wanted + step_of * half
    turn_ref[...] = one_hot(iota(turn_ref.shape, 1) == wanted)
    slot_ref[...] = one_hot(iota(slot_ref.shape, 1) == slot_of).astype(f32)

    row_index = iota((places * steps * half, 1), 0)
    source = jnp.zeros_like(row_index)
    adapter = jnp.zeros_like(row_index)
    for place in range(places):
        for slot in range(half):
            local = found[place * half + slot]
            here = (div(row_index, steps * half) == place) & (mod(row_index, half) == slot)
            source = jnp.where(here, local, source)
            adapter = jnp.where(here, adapter_ref[first + local], adapter)
    step_index = div(mod(row_index, steps * half), half)
    columns = iota((places * steps * half, total), 1)
    for h in range(heads):
        wanted = source * sh + step_index * heads + h
        span = slice(h * places * steps * half, (h + 1) * places * steps * half)
        back_v[span, :] = one_hot(columns == wanted)

    small_copies[3].wait()
    wanted = step_index * rows + source
    stream = dot(
        one_hot(iota((steps * rows, steps * rows), 1) == wanted),
        residual_ref[...].reshape(steps * rows, features),
    ).astype(bf16)
    for place, ref in enumerate((stay_ref, leave_ref)):
        span = slice(place * steps * half, (place + 1) * steps * half)
        ref[:, features + LANES :] = stream[span]

    pool_copy.wait()

    def block_rows(row, lo):
        return jnp.concatenate(
            [pool_v[table_ref[b, first + row], :, lo : lo + head] for b in range(table_blocks)],
            axis=0,
        )

    column = iota((sh, positions), 1)
    for row in range(rows):
        part = dot(query_rows[row * sh : (row + 1) * sh], block_rows(row, 0), ((1,), (1,)))
        part = jnp.where(column < lengths_ref[first + row], part * scale, f32(-1e30))
        scores_v[row * sh : (row + 1) * sh, :] = part

    scores = scores_v[...]
    top = jnp.max(scores, axis=1, keepdims=True)
    for value in fresh_scores:
        top = jnp.maximum(top, value)
    weights = jnp.exp(scores - top)
    fresh_weights = [jnp.exp(value - top) for value in fresh_scores]
    totals = jnp.sum(weights, axis=1, keepdims=True)
    for value in fresh_weights:
        totals = totals + value
    probs_v[...] = weights / totals

    for row in range(rows):
        span = slice(row * sh, (row + 1) * sh)
        attended_v[span, :] = dot(probs_v[span, :].astype(bf16), block_rows(row, head))
    attended = attended_v[...]
    for value, row in zip(fresh_weights, fresh_rows):
        share = (value / totals).astype(bf16).astype(f32)
        attended = attended + share * row[:, head:]
    attended = attended.astype(bf16)

    turned = dot(back_v[...], attended)
    count = places * steps * half
    mixed = jnp.concatenate(
        [turned[h * count : (h + 1) * count] for h in range(heads)], axis=1
    ).astype(bf16)

    small_copies[2].wait()
    wide = dot(mixed, down_ref[...].reshape(slots * rank, features), ((1,), (1,)))
    shrink = jnp.zeros((places * steps * half, rank), f32)
    for slot in range(slots):
        shrink = shrink + jnp.where(
            adapter == slot, wide[:, slot * rank : (slot + 1) * rank], 0.0
        )
    shrink = jnp.concatenate(
        [shrink, jnp.zeros((places * steps * half, LANES - rank), f32)], axis=1
    ).astype(bf16)

    group = steps * half
    for place, ref in enumerate((stay_ref, leave_ref)):
        span = slice(place * group, (place + 1) * group)
        ref[:, :features] = mixed[span]
        ref[:, features : features + LANES] = shrink[span]


def sort_kernel(turn_ref, stay_ref, came_ref, out_ref):
    out_ref[...] = dot(
        turn_ref[...], jnp.concatenate([stay_ref[...], came_ref[...]], axis=0)
    ).astype(bf16)


def sort_call(turn, stay, came):
    vmem = pl.BlockSpec(memory_space=pltpu.VMEM)
    return pl.pallas_call(
        sort_kernel,
        out_shape=pltpu.VMEM((turn.shape[0], stay.shape[1]), bf16),
        in_specs=[vmem] * 3,
        out_specs=vmem,
        compiler_params=pltpu.CompilerParams(vmem_limit_bytes=SMALL_BYTES),
        name="sort",
    )(turn, stay, came)


def message_kernel(rows_ref, came_ref, weight_ref, message_ref, *, partners):
    out_width = weight_ref.shape[1] // lax.axis_size("tensor")
    features = weight_ref.shape[0]
    spans = message_ref.shape[1] // (2 * out_width)
    here = lax.axis_index("tensor")
    partner = jnp.where(lax.axis_index("replica") == 0, partners[0], partners[1])
    half = message_ref.shape[0]
    mixed = rows_ref[:, :features]
    for span in range(spans):
        start = pl.multiple_of((here ^ (span * QUAD + partner)) * out_width, out_width)
        part = dot(mixed, weight_ref[:, pl.ds(start, out_width)]).astype(message_ref.dtype)
        for side in range(2):
            column = (2 * span + side) * out_width
            message_ref[:, column : column + out_width] = part[side * half : (side + 1) * half]
    rank = LANES // 2
    shrink = rows_ref[:, features : features + rank].astype(message_ref.dtype)
    message_ref[:, 2 * spans * out_width :] = jnp.concatenate([shrink[:half], shrink[half:]], axis=1)


def place_kernel(order_ref, lengths_ref, table_ref, pool_v, *refs, stayed):
    placed_ref, zero_v, edge_v, sem = refs[-4:]
    rows, table_blocks, block_size, _ = placed_ref.shape
    me = lax.axis_index("replica")
    zero_v[...] = jnp.zeros_like(zero_v)
    position = iota(zero_v.shape, 0)

    def step(j, count):
        request = order_ref[me * rows + j]
        length = lengths_ref[request]
        full = div(length, block_size)
        hit = (div(request, rows) == me) == stayed

        @pl.when(hit)
        def _():
            @pl.when(full < table_blocks)
            def _():
                block = table_ref[jnp.minimum(full, table_blocks - 1), request]
                kept = position < length - full * block_size
                edge_v[count] = jnp.where(kept, pool_v[block].astype(f32), 0.0).astype(bf16)

            for b in range(table_blocks):
                target = placed_ref.at[j, b]

                @pl.when(b < full)
                def _():
                    source = pool_v.at[table_ref[b, request]]
                    pltpu.make_async_copy(source, target, sem).start()

                @pl.when(b == full)
                def _():
                    pltpu.make_async_copy(edge_v.at[count], target, sem).start()

                @pl.when(b > full)
                def _():
                    pltpu.make_async_copy(zero_v, target, sem).start()

        return count + hit.astype(jnp.int32)

    lax.fori_loop(0, rows, step, jnp.int32(0))
    part = placed_ref.at[pl.ds(0, rows // 2)]
    pltpu.make_async_copy(part, part, sem).wait()


def in_hbm(value):
    return pltpu.with_memory_space_constraint(value, pltpu.HBM)


def attend_call(order, lengths, table, adapters, queries, fresh, down, residual, pool):
    steps, rows, features = queries.shape
    blocks, block_size, width = pool.shape
    table_blocks = table.shape[0]
    positions = table_blocks * block_size
    score_rows = rows * steps * features // (width // 2)
    smem = pl.BlockSpec(memory_space=pltpu.SMEM)
    vmem = pl.BlockSpec(memory_space=pltpu.VMEM)
    hbm = pl.BlockSpec(memory_space=pl.ANY)
    return pl.pallas_call(
        attend_kernel,
        out_shape=(
            pltpu.VMEM((steps * rows // 2, 2 * features + LANES), bf16),
            pltpu.VMEM((steps * rows // 2, 2 * features + LANES), bf16),
            pltpu.VMEM((steps * rows, steps * rows), bf16),
            pltpu.VMEM((steps * rows, 2 * down.shape[0]), f32),
            pltpu.VMEM(pool.shape, bf16),
        ),
        in_specs=[smem] * 4 + [hbm] * 5,
        out_specs=(vmem,) * 5,
        scratch_shapes=[
            pltpu.VMEM(queries.shape, bf16),
            pltpu.VMEM(fresh.shape, bf16),
            pltpu.VMEM(down.shape, bf16),
            pltpu.VMEM(residual.shape, bf16),
            pltpu.VMEM((score_rows, positions), f32),
            pltpu.VMEM((score_rows, positions), f32),
            pltpu.VMEM((score_rows, width // 2), f32),
            pltpu.VMEM((features // (width // 2) * steps * rows, score_rows), bf16),
            pltpu.SMEM((rows,), jnp.int32),
            pltpu.SMEM((rows,), jnp.int32),
            pltpu.SemaphoreType.DMA((4,)),
            pltpu.SemaphoreType.DMA,
        ],
        compiler_params=pltpu.CompilerParams(vmem_limit_bytes=2 * SMALL_BYTES),
        cost_estimate=pl.CostEstimate(
            flops=ATTEND_FLOPS, bytes_accessed=4 * pool.size, transcendentals=0
        ),
        name="attend",
    )(*(in_hbm(x) for x in (order, lengths, table, adapters, queries, fresh, down, residual, pool)))


def message_call(rows, came, weight, partners, dtype):
    tensor = lax.axis_size("tensor")
    columns = 2 * (tensor // QUAD) * (weight.shape[1] // tensor)
    vmem = pl.BlockSpec(memory_space=pltpu.VMEM)
    return pl.pallas_call(
        functools.partial(message_kernel, partners=partners),
        out_shape=pltpu.VMEM((rows.shape[0] // 2, columns + LANES), dtype),
        in_specs=[vmem] * 3,
        out_specs=vmem,
        compiler_params=pltpu.CompilerParams(vmem_limit_bytes=SMALL_BYTES),
        name="message",
    )(rows, came, weight)


def place_call(order, lengths, table, pool, rows, placed=None):
    smem = pl.BlockSpec(memory_space=pltpu.SMEM)
    vmem = pl.BlockSpec(memory_space=pltpu.VMEM)
    hbm = pl.BlockSpec(memory_space=pl.ANY)
    before = [] if placed is None else [placed]
    return pl.pallas_call(
        functools.partial(place_kernel, stayed=placed is None),
        out_shape=jax.ShapeDtypeStruct((rows, table.shape[0]) + pool.shape[1:], bf16),
        in_specs=[smem] * 3 + [vmem] + [hbm] * len(before),
        out_specs=hbm,
        scratch_shapes=[
            pltpu.VMEM(pool.shape[1:], bf16),
            pltpu.VMEM((rows // 2,) + pool.shape[1:], bf16),
            pltpu.SemaphoreType.DMA,
        ],
        input_output_aliases={4: 0} if before else {},
        compiler_params=pltpu.CompilerParams(vmem_limit_bytes=SMALL_BYTES),
        cost_estimate=pl.CostEstimate(flops=0, bytes_accessed=2 * pool.size, transcendentals=0),
        name="place",
    )(order, lengths, table, pool, *before)


def merge_kernel(*refs, spans):
    messages, outs, shrink_ref = refs[:-spans], refs[-spans:-1], refs[-1]
    width = (messages[0].shape[1] - LANES) // spans
    total = messages[0][:, width:]
    for ref in messages[1:]:
        total = total + ref[:, width:].astype(f32)
    shrink = total[:, (spans - 1) * width :]
    shrink_ref[...] = shrink
    for n, ref in enumerate(outs):
        ref[:, :width] = total[:, n * width : (n + 1) * width].astype(bf16)
        ref[:, width:] = shrink.astype(bf16)


def merge_call(messages, spans):
    rows, columns = messages[0].shape
    vmem = pl.BlockSpec(memory_space=pltpu.VMEM)
    width = (columns - LANES) // spans
    return pl.pallas_call(
        functools.partial(merge_kernel, spans=spans),
        out_shape=[pltpu.VMEM((rows, width + LANES), bf16)] * (spans - 1)
        + [pltpu.VMEM((rows, LANES), f32)],
        in_specs=[vmem] * len(messages),
        out_specs=[vmem] * spans,
        compiler_params=pltpu.CompilerParams(vmem_limit_bytes=SMALL_BYTES),
        cost_estimate=pl.CostEstimate(flops=MERGE_FLOPS, bytes_accessed=0, transcendentals=0),
        name="merge",
    )(*messages)


def finish_kernel(slot_ref, up_ref, other_up_ref, rows_ref, shrink_ref, *rest, home_count):
    home_refs, across_refs, out_ref = rest[:home_count], rest[home_count:-1], rest[-1]
    slots, rank, features = up_ref.shape
    width = 2 * features
    total, shrink = home_refs[0][:, :width], shrink_ref[...]
    for ref in home_refs[1:]:
        total = total + ref[:, :width].astype(f32)
    for ref in across_refs:
        total = total + ref[:, :width].astype(f32)
        shrink = shrink + ref[:, width:].astype(f32)
    total = jnp.concatenate([total[:, :features], total[:, features:]], axis=0)
    shrink = jnp.concatenate([shrink[:, :rank], shrink[:, LANES // 2 : LANES // 2 + rank]], axis=0)
    shrink = shrink.astype(bf16).astype(f32)
    result = total + rows_ref[:, features + LANES :].astype(f32)
    for side, up in enumerate((up_ref, other_up_ref)):
        wide = jnp.concatenate(
            [shrink * slot_ref[:, side * slots + n : side * slots + n + 1] for n in range(slots)],
            axis=1,
        ).astype(bf16)
        result = result + adapter_scale * dot(wide, up[...].reshape(slots * rank, features))
    out_ref[...] = result.astype(bf16).reshape(out_ref.shape)


def shards(
    queries,
    latest_key_value,
    residual,
    paged_cache_pool,
    adapter_down_weight,
    adapter_up_weight,
    output_weight,
    lengths,
    previous_block_table,
    request_order_after,
    request_adapter_index,
):
    steps, rows, features = queries.shape
    replicas = lax.axis_size("replica")
    tensor = lax.axis_size("tensor")
    blocks, _, block_size, width = paged_cache_pool.shape
    table_blocks = previous_block_table.shape[1]
    pool = paged_cache_pool.reshape(blocks, block_size, width)
    fresh = latest_key_value.reshape(steps, rows, width)
    swap = [(0, 1), (1, 0)]
    other_up = lax.ppermute(adapter_up_weight, "replica", swap)

    table = previous_block_table.T
    integers = (request_order_after, lengths, table, request_adapter_index)
    stay, leave, turn, slot, pool = attend_call(
        *integers, queries, fresh, adapter_down_weight, residual, pool
    )
    came = lax.ppermute(leave, "replica", swap)
    rows_in_order = sort_call(turn, stay, came)
    spans = tensor // QUAD
    def trade(message, partners):
        pairs = [
            (r * tensor + t, r * tensor + (t ^ partners[r]))
            for r in range(replicas)
            for t in range(tensor)
        ]
        return lax.ppermute(message, ("replica", "tensor"), pairs)

    collected = [
        trade(message_call(rows_in_order, came, output_weight, partners, bf16), partners)
        for partners in PARTNERS
    ]
    own = message_call(rows_in_order, came, output_weight, (0, 0), f32)
    home = [own] + collected
    other_pool = lax.ppermute(pool, "replica", swap)
    placed = place_call(*integers[:3], pool, rows)
    placed, own = lax.optimization_barrier((placed, own))
    home[0] = own
    *across, shrink = merge_call([own] + collected, spans)
    across = [trade(piece, (n * QUAD, n * QUAD)) for n, piece in enumerate(across, 1)]
    placed_cache = place_call(*integers[:3], other_pool, rows, placed)
    placed_cache, slot = lax.optimization_barrier((placed_cache, slot))
    vmem = pl.BlockSpec(memory_space=pltpu.VMEM)
    layer_out = pl.pallas_call(
        functools.partial(finish_kernel, home_count=len(home)),
        out_shape=jax.ShapeDtypeStruct((steps, rows, features), bf16),
        in_specs=[vmem] * (5 + len(home) + len(across)),
        out_specs=vmem,
        compiler_params=pltpu.CompilerParams(vmem_limit_bytes=SMALL_BYTES),
        name="finish",
    )(slot, adapter_up_weight, other_up, rows_in_order, shrink, *home, *across)
    return (layer_out, placed_cache.reshape(rows, table_blocks, 1, block_size, width))


def solution(mesh):
    in_specs = (
        P(None, ("groups", "replica"), "tensor"),
        P(None, ("groups", "replica"), "tensor", None),
        P(None, ("groups", "replica"), "tensor"),
        P(("groups", "replica"), "tensor", None, None),
        P(("groups", "replica"), None, "tensor"),
        P(("groups", "replica"), None, "tensor"),
        P("tensor", None),
        P("groups"),
        P("groups", None),
        P("groups"),
        P("groups"),
    )
    out_specs = (
        P(None, ("groups", "replica"), "tensor"),
        P(("groups", "replica"), None, "tensor", None, None),
    )
    return jax.shard_map(shards, mesh=mesh, in_specs=in_specs, out_specs=out_specs, check_vma=False)
```

```python
import functools

import jax
import jax.numpy as jnp
from jax import lax
from jax.experimental import pallas as pl
from jax.experimental.pallas import tpu as pltpu
from jax.sharding import PartitionSpec as P

adapter_scale = 2.0
bf16 = jnp.bfloat16
f32 = jnp.float32
LANES = 128
QUAD = 4
PARTNERS = ((3, 3), (2, 2), (1, 1))
ATTEND_FLOPS = 40_000_000_000
MERGE_FLOPS = 50_000_000_000
VMEM_BYTES = 56 * 1024 * 1024
SMALL_BYTES = 8 * 1024 * 1024


def iota(shape, dim):
    return lax.broadcasted_iota(jnp.int32, shape, dim)


def div(value, size):
    return value >> (size.bit_length() - 1) if size & (size - 1) == 0 else value // size


def mod(value, size):
    return value & (size - 1) if size & (size - 1) == 0 else value % size


def dot(a, b, contract=((1,), (0,))):
    return lax.dot_general(a, b, (contract, ((), ())), preferred_element_type=f32)


def one_hot(mask):
    return jnp.where(mask, 1.0, 0.0).astype(bf16)


def rank_rows(order_ref, found_ref, target_ref, holder, place, row_count, base):
    def step(j, count):
        request = order_ref[place * row_count + j]
        hit = div(request, row_count) == holder

        @pl.when(hit)
        def _():
            found_ref[base + count] = request - holder * row_count
            target_ref[base + count] = j

        return count + hit.astype(jnp.int32)

    lax.fori_loop(0, row_count, step, jnp.int32(0))


def attend_kernel(
    order_ref,
    lengths_ref,
    table_ref,
    adapter_ref,
    queries_hbm,
    fresh_hbm,
    down_hbm,
    residual_hbm,
    pool_ref,
    stay_ref,
    leave_ref,
    turn_ref,
    slot_ref,
    pool_v,
    queries_ref,
    fresh_ref,
    down_ref,
    residual_ref,
    scores_v,
    probs_v,
    attended_v,
    back_v,
    found,
    target,
    small_sem,
    pool_sem,
):
    steps, rows, features = queries_ref.shape
    blocks, block_size, width = pool_v.shape
    head = width // 2
    heads = features // head
    sh = steps * heads
    table_blocks = table_ref.shape[0]
    positions = table_blocks * block_size
    places = lengths_ref.shape[0] // rows
    half = rows // places
    slots, rank = down_ref.shape[:2]
    me = lax.axis_index("replica")
    first = me * rows

    small_copies = [
        pltpu.make_async_copy(source, target, small_sem.at[n])
        for n, (source, target) in enumerate(
            (
                (queries_hbm, queries_ref),
                (fresh_hbm, fresh_ref),
                (down_hbm, down_ref),
                (residual_hbm, residual_ref),
            )
        )
    ]
    pool_copy = pltpu.make_async_copy(pool_ref, pool_v, pool_sem)
    pool_copy.start()
    for copy in small_copies:
        copy.start()

    for place in range(places):
        rank_rows(order_ref, found, target, me, me if place == 0 else 1 - me, rows, place * half)

    small_copies[0].wait()
    small_copies[1].wait()
    stacked = jnp.concatenate(
        [
            queries_ref[s, :, h * head : (h + 1) * head]
            for s in range(steps)
            for h in range(heads)
        ],
        axis=0,
    )
    total = rows * sh
    out_row, in_row = iota((total, total), 0), iota((total, total), 1)
    turn = one_hot((div(out_row, sh) == mod(in_row, rows)) & (mod(out_row, sh) == div(in_row, rows)))
    turned = dot(turn, stacked)
    query_rows = turned.astype(bf16)
    spread = one_hot(div(iota((total, rows), 0), sh) == iota((total, rows), 1))
    scale = head ** (-0.5)
    fresh_rows = [dot(spread, fresh_ref[s]) for s in range(steps)]
    step_of = div(mod(iota((total, 1), 0), sh), heads)
    fresh_scores = []
    for s in range(steps):
        value = jnp.sum(turned * fresh_rows[s][:, :head], axis=1, keepdims=True) * scale
        fresh_scores.append(jnp.where(step_of >= s, value, f32(-1e30)))

    group = steps * half
    row = iota((2 * group, 1), 0)
    step_of, place_of = div(row, rows), mod(row, rows)
    wanted = jnp.zeros_like(row)
    slot_of = jnp.zeros_like(row)
    counts = [jnp.int32(0), jnp.int32(0)]
    for j in range(rows):
        request = order_ref[me * rows + j]
        away = jnp.where(div(request, rows) == me, 0, 1)
        count = jnp.where(away == 0, counts[0], counts[1])
        counts = [counts[0] + 1 - away, counts[1] + away]
        here = place_of == j
        wanted = jnp.where(here, away * group + count, wanted)
        slot_of = jnp.where(here, away * slots + adapter_ref[request], slot_of)
    wanted = wanted + step_of * half
    turn_ref[...] = one_hot(iota(turn_ref.shape, 1) == wanted)
    slot_ref[...] = one_hot(div(iota(slot_ref.shape, 1), rank) == slot_of).astype(f32)

    row_index = iota((places * steps * half, 1), 0)
    source = jnp.zeros_like(row_index)
    adapter = jnp.zeros_like(row_index)
    for place in range(places):
        for slot in range(half):
            local = found[place * half + slot]
            here = (div(row_index, steps * half) == place) & (mod(row_index, half) == slot)
            source = jnp.where(here, local, source)
            adapter = jnp.where(here, adapter_ref[first + local], adapter)
    step_index = div(mod(row_index, steps * half), half)
    columns = iota((places * steps * half, total), 1)
    for h in range(heads):
        wanted = source * sh + step_index * heads + h
        span = slice(h * places * steps * half, (h + 1) * places * steps * half)
        back_v[span, :] = one_hot(columns == wanted)

    small_copies[3].wait()
    wanted = step_index * rows + source
    stream = dot(
        one_hot(iota((steps * rows, steps * rows), 1) == wanted),
        residual_ref[...].reshape(steps * rows, features),
    ).astype(bf16)
    for place, ref in enumerate((stay_ref, leave_ref)):
        span = slice(place * steps * half, (place + 1) * steps * half)
        ref[:, features + LANES :] = stream[span]

    pool_copy.wait()

    def block_rows(row, lo):
        return jnp.concatenate(
            [pool_v[table_ref[b, first + row], :, lo : lo + head] for b in range(table_blocks)],
            axis=0,
        )

    column = iota((sh, positions), 1)
    for row in range(rows):
        part = dot(query_rows[row * sh : (row + 1) * sh], block_rows(row, 0), ((1,), (1,)))
        part = jnp.where(column < lengths_ref[first + row], part * scale, f32(-1e30))
        scores_v[row * sh : (row + 1) * sh, :] = part

    scores = scores_v[...]
    top = jnp.max(scores, axis=1, keepdims=True)
    for value in fresh_scores:
        top = jnp.maximum(top, value)
    weights = jnp.exp(scores - top)
    fresh_weights = [jnp.exp(value - top) for value in fresh_scores]
    totals = jnp.sum(weights, axis=1, keepdims=True)
    for value in fresh_weights:
        totals = totals + value
    probs_v[...] = weights / totals

    for row in range(rows):
        span = slice(row * sh, (row + 1) * sh)
        attended_v[span, :] = dot(probs_v[span, :].astype(bf16), block_rows(row, head))
    attended = attended_v[...]
    for value, row in zip(fresh_weights, fresh_rows):
        share = (value / totals).astype(bf16).astype(f32)
        attended = attended + share * row[:, head:]
    attended = attended.astype(bf16)

    turned = dot(back_v[...], attended)
    count = places * steps * half
    mixed = jnp.concatenate(
        [turned[h * count : (h + 1) * count] for h in range(heads)], axis=1
    ).astype(bf16)

    small_copies[2].wait()
    wide = dot(mixed, down_ref[...].reshape(slots * rank, features), ((1,), (1,)))
    shrink = jnp.zeros((places * steps * half, rank), f32)
    for slot in range(slots):
        shrink = shrink + jnp.where(
            adapter == slot, wide[:, slot * rank : (slot + 1) * rank], 0.0
        )
    shrink = jnp.concatenate(
        [shrink, jnp.zeros((places * steps * half, LANES - rank), f32)], axis=1
    ).astype(bf16)

    group = steps * half
    for place, ref in enumerate((stay_ref, leave_ref)):
        span = slice(place * group, (place + 1) * group)
        ref[:, :features] = mixed[span]
        ref[:, features : features + LANES] = shrink[span]


def sort_kernel(turn_ref, stay_ref, came_ref, out_ref):
    out_ref[...] = dot(
        turn_ref[...], jnp.concatenate([stay_ref[...], came_ref[...]], axis=0)
    ).astype(bf16)


def sort_call(turn, stay, came):
    vmem = pl.BlockSpec(memory_space=pltpu.VMEM)
    return pl.pallas_call(
        sort_kernel,
        out_shape=pltpu.VMEM((turn.shape[0], stay.shape[1]), bf16),
        in_specs=[vmem] * 3,
        out_specs=vmem,
        compiler_params=pltpu.CompilerParams(vmem_limit_bytes=SMALL_BYTES),
        name="sort",
    )(turn, stay, came)


def message_kernel(rows_ref, came_ref, weight_ref, message_ref, *, partners):
    out_width = weight_ref.shape[1] // lax.axis_size("tensor")
    features = weight_ref.shape[0]
    spans = message_ref.shape[1] // (2 * out_width)
    here = lax.axis_index("tensor")
    partner = jnp.where(lax.axis_index("replica") == 0, partners[0], partners[1])
    half = message_ref.shape[0]
    mixed = rows_ref[:, :features]
    for span in range(spans):
        start = pl.multiple_of((here ^ (span * QUAD + partner)) * out_width, out_width)
        part = dot(mixed, weight_ref[:, pl.ds(start, out_width)]).astype(message_ref.dtype)
        for side in range(2):
            column = (2 * span + side) * out_width
            message_ref[:, column : column + out_width] = part[side * half : (side + 1) * half]
    rank = LANES // 2
    shrink = rows_ref[:, features : features + rank].astype(message_ref.dtype)
    message_ref[:, 2 * spans * out_width :] = jnp.concatenate([shrink[:half], shrink[half:]], axis=1)


def place_kernel(order_ref, lengths_ref, table_ref, pool_v, *refs, stayed):
    placed_ref, zero_v, edge_v, sem = refs[-4:]
    rows, table_blocks, block_size, _ = placed_ref.shape
    me = lax.axis_index("replica")
    zero_v[...] = jnp.zeros_like(zero_v)
    position = iota(zero_v.shape, 0)

    def step(j, count):
        request = order_ref[me * rows + j]
        length = lengths_ref[request]
        full = div(length, block_size)
        hit = (div(request, rows) == me) == stayed

        @pl.when(hit)
        def _():
            @pl.when(full < table_blocks)
            def _():
                block = table_ref[jnp.minimum(full, table_blocks - 1), request]
                kept = position < length - full * block_size
                edge_v[count] = jnp.where(kept, pool_v[block].astype(f32), 0.0).astype(bf16)

            for b in range(table_blocks):
                target = placed_ref.at[j, b]

                @pl.when(b < full)
                def _():
                    source = pool_v.at[table_ref[b, request]]
                    pltpu.make_async_copy(source, target, sem).start()

                @pl.when(b == full)
                def _():
                    pltpu.make_async_copy(edge_v.at[count], target, sem).start()

                @pl.when(b > full)
                def _():
                    pltpu.make_async_copy(zero_v, target, sem).start()

        return count + hit.astype(jnp.int32)

    lax.fori_loop(0, rows, step, jnp.int32(0))
    part = placed_ref.at[pl.ds(0, rows // 2)]
    pltpu.make_async_copy(part, part, sem).wait()


def in_hbm(value):
    return pltpu.with_memory_space_constraint(value, pltpu.HBM)


def attend_call(order, lengths, table, adapters, queries, fresh, down, residual, pool):
    steps, rows, features = queries.shape
    blocks, block_size, width = pool.shape
    table_blocks = table.shape[0]
    positions = table_blocks * block_size
    score_rows = rows * steps * features // (width // 2)
    smem = pl.BlockSpec(memory_space=pltpu.SMEM)
    vmem = pl.BlockSpec(memory_space=pltpu.VMEM)
    hbm = pl.BlockSpec(memory_space=pl.ANY)
    return pl.pallas_call(
        attend_kernel,
        out_shape=(
            pltpu.VMEM((steps * rows // 2, 2 * features + LANES), bf16),
            pltpu.VMEM((steps * rows // 2, 2 * features + LANES), bf16),
            pltpu.VMEM((steps * rows, steps * rows), bf16),
            pltpu.VMEM((steps * rows, 2 * down.shape[0] * down.shape[1]), f32),
            pltpu.VMEM(pool.shape, bf16),
        ),
        in_specs=[smem] * 4 + [hbm] * 5,
        out_specs=(vmem,) * 5,
        scratch_shapes=[
            pltpu.VMEM(queries.shape, bf16),
            pltpu.VMEM(fresh.shape, bf16),
            pltpu.VMEM(down.shape, bf16),
            pltpu.VMEM(residual.shape, bf16),
            pltpu.VMEM((score_rows, positions), f32),
            pltpu.VMEM((score_rows, positions), f32),
            pltpu.VMEM((score_rows, width // 2), f32),
            pltpu.VMEM((features // (width // 2) * steps * rows, score_rows), bf16),
            pltpu.SMEM((rows,), jnp.int32),
            pltpu.SMEM((rows,), jnp.int32),
            pltpu.SemaphoreType.DMA((4,)),
            pltpu.SemaphoreType.DMA,
        ],
        compiler_params=pltpu.CompilerParams(vmem_limit_bytes=2 * SMALL_BYTES),
        cost_estimate=pl.CostEstimate(
            flops=ATTEND_FLOPS, bytes_accessed=4 * pool.size, transcendentals=0
        ),
        name="attend",
    )(*(in_hbm(x) for x in (order, lengths, table, adapters, queries, fresh, down, residual, pool)))


def message_call(rows, came, weight, partners, dtype):
    tensor = lax.axis_size("tensor")
    columns = 2 * (tensor // QUAD) * (weight.shape[1] // tensor)
    vmem = pl.BlockSpec(memory_space=pltpu.VMEM)
    return pl.pallas_call(
        functools.partial(message_kernel, partners=partners),
        out_shape=pltpu.VMEM((rows.shape[0] // 2, columns + LANES), dtype),
        in_specs=[vmem] * 3,
        out_specs=vmem,
        compiler_params=pltpu.CompilerParams(vmem_limit_bytes=SMALL_BYTES),
        name="message",
    )(rows, came, weight)


def place_call(order, lengths, table, pool, rows, placed=None):
    smem = pl.BlockSpec(memory_space=pltpu.SMEM)
    vmem = pl.BlockSpec(memory_space=pltpu.VMEM)
    hbm = pl.BlockSpec(memory_space=pl.ANY)
    before = [] if placed is None else [placed]
    return pl.pallas_call(
        functools.partial(place_kernel, stayed=placed is None),
        out_shape=jax.ShapeDtypeStruct((rows, table.shape[0]) + pool.shape[1:], bf16),
        in_specs=[smem] * 3 + [vmem] + [hbm] * len(before),
        out_specs=hbm,
        scratch_shapes=[
            pltpu.VMEM(pool.shape[1:], bf16),
            pltpu.VMEM((rows // 2,) + pool.shape[1:], bf16),
            pltpu.SemaphoreType.DMA,
        ],
        input_output_aliases={4: 0} if before else {},
        compiler_params=pltpu.CompilerParams(vmem_limit_bytes=SMALL_BYTES),
        cost_estimate=pl.CostEstimate(flops=0, bytes_accessed=2 * pool.size, transcendentals=0),
        name="place",
    )(order, lengths, table, pool, *before)


def merge_kernel(*refs, spans):
    messages, outs, shrink_ref = refs[:-spans], refs[-spans:-1], refs[-1]
    width = (messages[0].shape[1] - LANES) // spans
    total = messages[0][:, width:]
    for ref in messages[1:]:
        total = total + ref[:, width:].astype(f32)
    shrink = total[:, (spans - 1) * width :]
    shrink_ref[...] = shrink
    for n, ref in enumerate(outs):
        ref[:, :width] = total[:, n * width : (n + 1) * width].astype(bf16)
        ref[:, width:] = shrink.astype(bf16)


def merge_call(messages, spans):
    rows, columns = messages[0].shape
    vmem = pl.BlockSpec(memory_space=pltpu.VMEM)
    width = (columns - LANES) // spans
    return pl.pallas_call(
        functools.partial(merge_kernel, spans=spans),
        out_shape=[pltpu.VMEM((rows, width + LANES), bf16)] * (spans - 1)
        + [pltpu.VMEM((rows, LANES), f32)],
        in_specs=[vmem] * len(messages),
        out_specs=[vmem] * spans,
        compiler_params=pltpu.CompilerParams(vmem_limit_bytes=SMALL_BYTES),
        cost_estimate=pl.CostEstimate(flops=MERGE_FLOPS, bytes_accessed=0, transcendentals=0),
        name="merge",
    )(*messages)


def base_kernel(rows_ref, *rest):
    home_refs, base_ref = rest[:-1], rest[-1]
    features = base_ref.shape[1]
    width = 2 * features
    total = home_refs[0][:, :width]
    for ref in home_refs[1:]:
        total = total + ref[:, :width].astype(f32)
    total = jnp.concatenate([total[:, :features], total[:, features:]], axis=0)
    base_ref[...] = total + rows_ref[:, features + LANES :].astype(f32)


def base_call(rows, home, features):
    vmem = pl.BlockSpec(memory_space=pltpu.VMEM)
    return pl.pallas_call(
        base_kernel,
        out_shape=pltpu.VMEM((rows.shape[0], features), f32),
        in_specs=[vmem] * (1 + len(home)),
        out_specs=vmem,
        compiler_params=pltpu.CompilerParams(vmem_limit_bytes=SMALL_BYTES),
        name="base",
    )(rows, *home)


def finish_kernel(slot_ref, up_ref, other_up_ref, base_ref, shrink_ref, *rest):
    across_refs, out_ref = rest[:-1], rest[-1]
    slots, rank, features = up_ref.shape
    width = 2 * features
    shrink = shrink_ref[...]
    for ref in across_refs:
        shrink = shrink + ref[:, width:].astype(f32)
    turned = pltpu.roll(shrink, LANES // 2, 1)
    left = iota(shrink.shape, 1) < LANES // 2
    shrink = jnp.concatenate(
        [jnp.where(left, shrink, turned), jnp.where(left, turned, shrink)], axis=0
    )
    shrink = shrink.astype(bf16).astype(f32)
    span = slots * rank
    wide = jnp.concatenate([shrink] * (2 * span // LANES), axis=1) * slot_ref[...]
    wide = wide.astype(bf16)
    result = base_ref[...]
    for ref in across_refs:
        result = result + jnp.concatenate(
            [ref[:, :features], ref[:, features:width]], axis=0
        ).astype(f32)
    for side, up in enumerate((up_ref, other_up_ref)):
        raised = dot(wide[:, side * span : (side + 1) * span], up[...].reshape(span, features))
        result = result + adapter_scale * raised
    out_ref[...] = result.astype(bf16).reshape(out_ref.shape)


def shards(
    queries,
    latest_key_value,
    residual,
    paged_cache_pool,
    adapter_down_weight,
    adapter_up_weight,
    output_weight,
    lengths,
    previous_block_table,
    request_order_after,
    request_adapter_index,
):
    steps, rows, features = queries.shape
    replicas = lax.axis_size("replica")
    tensor = lax.axis_size("tensor")
    blocks, _, block_size, width = paged_cache_pool.shape
    table_blocks = previous_block_table.shape[1]
    pool = paged_cache_pool.reshape(blocks, block_size, width)
    fresh = latest_key_value.reshape(steps, rows, width)
    swap = [(0, 1), (1, 0)]
    other_up = lax.ppermute(adapter_up_weight, "replica", swap)

    table = previous_block_table.T
    integers = (request_order_after, lengths, table, request_adapter_index)
    stay, leave, turn, slot, pool = attend_call(
        *integers, queries, fresh, adapter_down_weight, residual, pool
    )
    came = lax.ppermute(leave, "replica", swap)
    rows_in_order = sort_call(turn, stay, came)
    spans = tensor // QUAD
    def trade(message, partners):
        pairs = [
            (r * tensor + t, r * tensor + (t ^ partners[r]))
            for r in range(replicas)
            for t in range(tensor)
        ]
        return lax.ppermute(message, ("replica", "tensor"), pairs)

    collected = [
        trade(message_call(rows_in_order, came, output_weight, partners, bf16), partners)
        for partners in PARTNERS
    ]
    own = message_call(rows_in_order, came, output_weight, (0, 0), f32)
    home = [own] + collected
    other_pool = lax.ppermute(pool, "replica", swap)
    placed = place_call(*integers[:3], pool, rows)
    placed, own = lax.optimization_barrier((placed, own))
    home[0] = own
    *across, shrink = merge_call([own] + collected, spans)
    across = [trade(piece, (n * QUAD, n * QUAD)) for n, piece in enumerate(across, 1)]
    placed_cache = place_call(*integers[:3], other_pool, rows, placed)
    placed_cache, own = lax.optimization_barrier((placed_cache, own))
    base = base_call(rows_in_order, [own] + collected, features)
    vmem = pl.BlockSpec(memory_space=pltpu.VMEM)
    layer_out = pl.pallas_call(
        finish_kernel,
        out_shape=jax.ShapeDtypeStruct((steps, rows, features), bf16),
        in_specs=[vmem] * (5 + len(across)),
        out_specs=vmem,
        compiler_params=pltpu.CompilerParams(vmem_limit_bytes=SMALL_BYTES),
        name="finish",
    )(slot, adapter_up_weight, other_up, base, shrink, *across)
    return (layer_out, placed_cache.reshape(rows, table_blocks, 1, block_size, width))


def solution(mesh):
    in_specs = (
        P(None, ("groups", "replica"), "tensor"),
        P(None, ("groups", "replica"), "tensor", None),
        P(None, ("groups", "replica"), "tensor"),
        P(("groups", "replica"), "tensor", None, None),
        P(("groups", "replica"), None, "tensor"),
        P(("groups", "replica"), None, "tensor"),
        P("tensor", None),
        P("groups"),
        P("groups", None),
        P("groups"),
        P("groups"),
    )
    out_specs = (
        P(None, ("groups", "replica"), "tensor"),
        P(("groups", "replica"), None, "tensor", None, None),
    )
    return jax.shard_map(shards, mesh=mesh, in_specs=in_specs, out_specs=out_specs, check_vma=False)
```
